32 devices in a mesh: group: 2 (over y), index: 8 (over z, x), query: 2 (over core).
Axes of the slice: x: 2, y: 2, z: 4, core: 2. Of those that a mesh axis runs over, the one named last changes fastest.
Arguments:
- queries: bfloat16 [128, 32, 128], P(('group', 'index', 'query')), parts along dimension 0, may hold values from -6 to 6
- cand_owner: int32 [128, 8], P(('group', 'index', 'query')), parts along dimension 0, may hold values from 0 to 7, as said below
- cand_local: int32 [128, 8], P(('group', 'index', 'query')), parts along dimension 0, may hold values from 0 to 127
- centroids: bfloat16 [2048, 128], P('index'), may hold values from -0.5 to 0.5
- passage_codes: int32 [1024, 64], P('index'), may hold values from 0 to 2047, as said below
- residuals: bfloat16 [1024, 64, 128], P('index'), may hold values from -0.25 to 0.25
- passage_lengths: int32 [1024], P('index'), may hold values from 16 to 64, as said below
Outputs:
- exact_scores: float32 [128, 8], P(('group', 'index', 'query')), parts along dimension 0
- centroid_scores: float32 [128, 8], P(('group', 'index', 'query')), parts along dimension 0
The draws below stay inside these ranges and needn't reach their ends.
There are 2 independent parts, one for each index of `group`. The reference program is written for one: setup_inputs(seed, part) draws one part's arguments, and reference() takes and returns one part's arrays. A program takes and returns all parts, laid end to end along the dimension named above; an argument that names none is the same for every part. Nothing has to cross between parts.
Inputs may be any that keep to these rules, and one draw needn't show every extreme that they name: `cand_owner`: in each aligned block of 4 rows (the queries of one device) no index device is named more than 8 times, and in every block some index device is named exactly 8 times. `passage_codes`: in each aligned block of 128 rows (the passages of one index device), no range of 256 centroid numbers starting at a multiple of 256 is named by more than 1536 tokens, and in every block one such range is named by exactly 1536 tokens. `passage_lengths`: some passage of every index device has 64 tokens.
All inputs are finite; a program needn't handle non-finite values.
Results may differ from the reference program's by a relative error of at most 0.00037.
Values may be sent and summed in bfloat16 or wider, within the bound.
No kernel may reach another device: no remote copies, remote signals or barrier semaphores. Data moves between devices by JAX's collectives and lax.ppermute only.
A program may use at most 128 MiB of HBM per device.

```python
import jax
import jax.numpy as jnp
from jax import lax

DIM = 128
QTOK = 32
LEN = 64
K = 8
CENT_DEV = 256
Q_DEV = 4
P_DEV = 128
NCENT = 2048
QUERIES = 64
PASSAGES = 1024
CANDIDATE_LIMIT = 8
CODE_TOKEN_LIMIT = 1536


def draw_cand_owner(key, part):
    key = jax.random.fold_in(key, 5)
    proprietors = PASSAGES // P_DEV
    slot_count = proprietors * CANDIDATE_LIMIT
    count = Q_DEV * K
    nblocks = QUERIES // Q_DEV
    popularity = jax.random.randint(jax.random.fold_in(key, 1), (proprietors,), 0, 2)
    block_keys = jax.random.split(jax.random.fold_in(key, 2), nblocks)

    def one_block(block_key):
        key_full, key_standing, key_order = jax.random.split(block_key, 3)
        complete_proprietor = jax.random.randint(key_full, (), 0, proprietors)
        device_rank = jax.random.permutation(key_standing, slot_count).astype(jnp.int32)
        slot_proprietor = jnp.arange(slot_count, dtype=jnp.int32) // CANDIDATE_LIMIT
        score_value = (slot_proprietor != complete_proprietor).astype(jnp.int32) * (4 * slot_count) + (1 - popularity[slot_proprietor]) * (slot_count // 2) + device_rank
        order = jnp.argsort(score_value, stable=True)
        chosen = (order[:count] // CANDIDATE_LIMIT).astype(jnp.int32)
        return chosen[jax.random.permutation(key_order, count)].reshape(Q_DEV, K)
    return jax.vmap(one_block)(block_keys).reshape(QUERIES, K).astype(jnp.int32)


def draw_passage_codes(key, part):
    key = jax.random.fold_in(key, 9)
    proprietors = PASSAGES // P_DEV
    count = P_DEV * LEN
    slot_count = proprietors * CODE_TOKEN_LIMIT
    block_keys = jax.random.split(key, proprietors)

    def one_block(block_key):
        key_full, key_standing, key_order, key_row = jax.random.split(block_key, 4)
        complete_keeper = jax.random.randint(key_full, (), 0, proprietors)
        device_rank = jax.random.permutation(key_standing, slot_count).astype(jnp.int32)
        slot_keeper = jnp.arange(slot_count, dtype=jnp.int32) // CODE_TOKEN_LIMIT
        score_value = (slot_keeper != complete_keeper).astype(jnp.int32) * (2 * slot_count) + device_rank
        order = jnp.argsort(score_value, stable=True)
        holders = (order[:count] // CODE_TOKEN_LIMIT).astype(jnp.int32)
        holders = holders[jax.random.permutation(key_order, count)]
        rows = jax.random.randint(key_row, (count,), 0, CENT_DEV)
        return (holders * CENT_DEV + rows).reshape(P_DEV, LEN)
    return jax.vmap(one_block)(block_keys).reshape(PASSAGES, LEN).astype(jnp.int32)


def draw_passage_lengths(key, part):
    key = jax.random.fold_in(key, 7)
    lengths = jax.random.randint(key, (PASSAGES,), LEN // 4, LEN + 1)
    return lengths.at[::P_DEV].set(LEN).astype(jnp.int32)


def touch_ends(result, stream_key, least, high):
    spot = [jax.random.randint(jax.random.fold_in(stream_key, axis), (), 0, length) for axis, length in enumerate(result.shape)]
    longest = result.shape.index(max(result.shape))
    next_to = spot[:longest] + [(spot[longest] + 1) % result.shape[longest]] + spot[longest + 1:]
    return result.at[tuple(spot)].set(least).at[tuple(next_to)].set(high)


def levels(rng, dims, pieces, smallest, high):
    gain, own = 1.0, jax.random.fold_in(rng, 6)
    for dim, parts in pieces:
        heights = jnp.exp(jax.random.uniform(jax.random.fold_in(own, dim), (parts,), jnp.float32, smallest / len(pieces), high / len(pieces)))
        gain = gain * jnp.repeat(heights, dims[dim] // parts).reshape([-1 if axis == dim else 1 for axis in range(len(dims))])
    return gain


def noise(own_key, dims, width, bound, cuts=(), kind=jnp.bfloat16):
    drawn = width * jax.random.normal(own_key, dims, jnp.float32)
    if cuts:
        drawn = drawn * levels(own_key, dims, cuts, -0.22, 0.18)
    return jnp.clip(drawn, -bound, bound).astype(kind)


def setup_inputs(seed: int = 0, part: int = 0) -> dict:
    key_list = jax.random.split(jax.random.key(seed), 8)
    part_keys = jax.random.split(jax.random.fold_in(key_list[7], part), 8)
    queries = noise(part_keys[0], (QUERIES, QTOK, DIM), 1.0, 6.0, ((0, 16),))
    cand_owner = draw_cand_owner(jax.random.fold_in(jax.random.fold_in(key_list[7], part), 71), part)
    cand_local = touch_ends(jax.random.randint(part_keys[2], (QUERIES, K), 0, P_DEV), jax.random.fold_in(part_keys[2], 1), 0, P_DEV - 1).astype(jnp.int32)
    centroids = noise(key_list[3], (NCENT, DIM), 0.09, 0.5, ((0, 8),))
    passage_codes = draw_passage_codes(jax.random.fold_in(key_list[7], 71), part)
    residuals = noise(key_list[5], (PASSAGES, LEN, DIM), 0.04, 0.25, ((0, 8),))
    passage_lengths = draw_passage_lengths(jax.random.fold_in(key_list[7], 71), part)
    return dict(queries=queries, cand_owner=cand_owner, cand_local=cand_local, centroids=centroids, passage_codes=passage_codes, residuals=residuals, passage_lengths=passage_lengths)


def normalize_rows(values):
    wide = values.astype(jnp.float32)
    return (wide * lax.rsqrt(lax.optimization_barrier(jnp.sum(wide * wide, axis=-1, keepdims=True)) + 1e-06)).astype(jnp.bfloat16)

def scores_of(tokens, documents, lengths):
    sims = jnp.einsum('qid,qkjd->qkij', tokens.astype(jnp.float32), documents.astype(jnp.float32))
    live = jnp.arange(LEN, dtype=jnp.int32)[None, None, None, :] < lengths[:, :, None, None]
    return lax.optimization_barrier(jnp.sum(lax.optimization_barrier(jnp.max(jnp.where(live, sims, -1000000000.0), axis=3)), axis=2))

def reference(queries, cand_owner, cand_local, centroids, passage_codes, residuals, passage_lengths):
    qnorm = normalize_rows(queries)
    passage = (cand_owner * P_DEV + cand_local).astype(jnp.int32)
    blocks = QUERIES // Q_DEV

    def one_block(operands):
        tokens, picks = operands
        codes = passage_codes[picks]
        lengths = passage_lengths[picks]
        cent_rows = centroids[codes]
        decoded = normalize_rows(cent_rows.astype(jnp.float32) + residuals[picks].astype(jnp.float32))
        return (scores_of(tokens, decoded, lengths), scores_of(tokens, cent_rows, lengths))
    exact, approx = lax.map(one_block, (qnorm.reshape(blocks, Q_DEV, QTOK, DIM), passage.reshape(blocks, Q_DEV, K)))
    return (exact.reshape(QUERIES, K), approx.reshape(QUERIES, K))
```

```python
import functools

import jax
import jax.numpy as jnp
from jax import lax
from jax.experimental import pallas as pl
from jax.experimental.pallas import tpu as pltpu
from jax.sharding import PartitionSpec as P

EPS = 1e-06
PAD = 16
VMEM_LIMIT = 56 * 1024 * 1024


def normalize(wide):
    return wide * lax.rsqrt(jnp.sum(wide * wide, axis=-1, keepdims=True) + EPS)


def pack_kernel(owner_ref, local_ref, queries_ref, cent_ref, out_ref, count_ref, req_ref):
    peers = out_ref.shape[0]
    q_dev, per_query = owner_ref.shape
    qrows = queries_ref.shape[0] * queries_ref.shape[1]
    dim = queries_ref.shape[2]
    half = cent_ref.shape[0] // lax.axis_size("query")
    core = lax.axis_index("query")

    def clear(i, carry):
        count_ref[i] = 0
        return carry

    lax.fori_loop(0, peers, clear, 0)
    row = lax.broadcasted_iota(jnp.int32, req_ref.shape, 0)
    lane = lax.broadcasted_iota(jnp.int32, req_ref.shape, 1)
    req = jnp.full(req_ref.shape, -1, jnp.int32)
    for q in range(q_dev):
        for k in range(per_query):
            owner = owner_ref[q, k]
            slot = count_ref[owner]
            count_ref[owner] = slot + 1
            here = row == owner
            req = jnp.where(here & (lane == slot), local_ref[q, k], req)
            req = jnp.where(here & (lane == slot + dim // 2), q * per_query + k, req)
    req_ref[...] = req.astype(jnp.float32)
    qnorm = normalize(queries_ref[...].reshape(qrows, dim).astype(jnp.float32)).astype(jnp.bfloat16)
    cent = cent_ref[pl.ds(pl.multiple_of(core * half, 16), half), :]

    def send(d, carry):
        out_ref[d, :qrows, :] = qnorm
        out_ref[d, qrows : qrows + half, :] = cent
        out_ref[d, qrows + half :, :] = jnp.broadcast_to(req_ref[pl.ds(d, 1), :], (PAD, dim)).astype(
            jnp.bfloat16
        )
        return carry

    lax.fori_loop(0, peers, send, 0, unroll=peers <= 16)


def score_kernel(
    slots,
    q_dev,
    per_query,
    qtok,
    req_ref,
    length_ref,
    recv_ref,
    other_ref,
    codes_ref,
    resid_ref,
    out_ref,
    table_ref,
    dec_ref,
    cent_ref,
):
    peers, half, dim = other_ref.shape
    qrows = q_dev * qtok
    seq = codes_ref.shape[0]
    shard = 2 * half
    core = lax.axis_index("query")

    def place(h, carry):
        cols = pl.ds(pl.multiple_of(h * dim, dim), dim)
        table_ref[:half, cols] = recv_ref[h, qrows : qrows + half, :]
        table_ref[half:, cols] = other_ref[h]
        return carry

    lax.fori_loop(0, peers, place, 0, unroll=peers <= 16)
    lane = lax.broadcasted_iota(jnp.int32, (seq, dim), 1)
    token = lax.broadcasted_iota(jnp.int32, (seq, dim), 0)
    row8 = lax.broadcasted_iota(jnp.int32, (2 * q_dev, dim), 0)
    lane8 = lax.broadcasted_iota(jnp.int32, (2 * q_dev, dim), 1)
    lane1 = lax.broadcasted_iota(jnp.int32, (1, dim), 1)

    def block(b, carry):
        hot, high = [], []
        for s in range(slots):
            p = jnp.maximum(req_ref[b, s], 0)
            code = jnp.take_along_axis(codes_ref[...], jnp.full((seq, dim), p, jnp.int32), axis=1)
            low = (code % shard) ^ (core * half)
            high.append(code // shard)
            hot.append(
                jnp.concatenate([low == lane + i * dim for i in range(shard // dim)], axis=1)
                .astype(jnp.float32)
                .astype(jnp.bfloat16)
            )
        hot = jnp.concatenate(hot, axis=0)
        high = jnp.concatenate(high, axis=0)

        def pick(h, cent):
            cols = pl.ds(pl.multiple_of(2 * h * dim, 2 * dim), 2 * dim)
            rows = jnp.dot(hot, table_ref[:, cols], preferred_element_type=jnp.float32)
            cent = jnp.where(high == 2 * h, rows[:, :dim], cent)
            return jnp.where(high == 2 * h + 1, rows[:, dim:], cent)

        cent = lax.fori_loop(
            0, peers // 2, pick, jnp.zeros((slots * seq, dim), jnp.float32), unroll=peers <= 16
        )
        cent_ref[...] = cent.astype(jnp.bfloat16)
        for s in range(slots):
            p = jnp.maximum(req_ref[b, s], 0)
            v = cent[s * seq : (s + 1) * seq] + resid_ref[p].astype(jnp.float32)
            dec_ref[s * seq : (s + 1) * seq, :] = normalize(v).astype(jnp.bfloat16)
        query = recv_ref[b, :qrows, :]
        nt = (((1,), (1,)), ((), ()))
        exact = lax.dot_general(dec_ref[...], query, nt, preferred_element_type=jnp.float32)
        approx = lax.dot_general(cent_ref[...], query, nt, preferred_element_type=jnp.float32)
        total = jnp.zeros((2 * q_dev, dim), jnp.float32)
        for s in range(slots):
            p = jnp.maximum(req_ref[b, s], 0)
            c = req_ref[b, s + dim // 2]
            q, k = c // per_query, c % per_query
            live = token < length_ref[p]
            mine = lane1 // qtok == q
            for off, sims in ((0, exact), (q_dev, approx)):
                best = jnp.max(
                    jnp.where(live, sims[s * seq : (s + 1) * seq], -1000000000.0), axis=0, keepdims=True
                )
                score = jnp.sum(jnp.where(mine, best, 0.0), axis=1, keepdims=True)
                total += jnp.where((row8 == q + off) & (lane8 == k) & (c >= 0), score, 0.0)
        out_ref[b] = total
        return carry

    lax.fori_loop(0, peers, block, 0)


def body(queries, cand_owner, cand_local, centroids, passage_codes, residuals, passage_lengths):
    peers = lax.axis_size("index")
    cores = lax.axis_size("query")
    q_dev, per_query = cand_owner.shape
    count = q_dev * per_query
    slots = max(2, (2 * count + peers - 1) // peers)
    seq, dim = residuals.shape[1:]
    qtok = queries.shape[1]
    qrows = q_dev * qtok
    half = centroids.shape[0] // cores
    rows = qrows + half + PAD
    vmem = pl.BlockSpec(memory_space=pltpu.VMEM)
    smem = pl.BlockSpec(memory_space=pltpu.SMEM)
    params = pltpu.CompilerParams(vmem_limit_bytes=VMEM_LIMIT)
    packed = pl.pallas_call(
        pack_kernel,
        out_shape=jax.ShapeDtypeStruct((peers, rows, dim), jnp.bfloat16),
        in_specs=[smem, smem, vmem, vmem],
        out_specs=vmem,
        scratch_shapes=[pltpu.SMEM((peers,), jnp.int32), pltpu.VMEM((peers, dim), jnp.float32)],
        compiler_params=params,
    )(cand_owner, cand_local, queries, centroids)
    recv = lax.all_to_all(packed, "index", split_axis=0, concat_axis=0, tiled=True)
    other = lax.ppermute(recv[:, qrows : qrows + half, :], "query", [(0, 1), (1, 0)])
    requests = recv[:, qrows + half, :].astype(jnp.int32)
    scores = pl.pallas_call(
        functools.partial(score_kernel, slots, q_dev, per_query, qtok),
        out_shape=jax.ShapeDtypeStruct((peers, 2 * q_dev, dim), jnp.float32),
        in_specs=[smem, smem, vmem, vmem, vmem, vmem],
        out_specs=vmem,
        scratch_shapes=[
            pltpu.VMEM((cores * half, peers * dim), jnp.bfloat16),
            pltpu.VMEM((slots * seq, dim), jnp.bfloat16),
            pltpu.VMEM((slots * seq, dim), jnp.bfloat16),
        ],
        compiler_params=params,
    )(requests, passage_lengths, recv, other, passage_codes.T, residuals)
    back = lax.all_to_all(scores, "index", split_axis=0, concat_axis=0, tiled=True)
    result = jnp.sum(back[:, :, :per_query], axis=0)
    return result[:q_dev], result[q_dev:]


def solution(mesh):
    in_specs = (
        P(("group", "index", "query"), None, None),
        P(("group", "index", "query"), None),
        P(("group", "index", "query"), None),
        P("index", None),
        P("index", None),
        P("index", None, None),
        P("index"),
    )
    out_specs = (P(("group", "index", "query"), None), P(("group", "index", "query"), None))
    return jax.shard_map(body, mesh=mesh, in_specs=in_specs, out_specs=out_specs, check_vma=False)
```

```python
import functools

import jax
import jax.numpy as jnp
from jax import lax
from jax.experimental import pallas as pl
from jax.experimental.pallas import tpu as pltpu
from jax.sharding import PartitionSpec as P

EPS = 1e-06
PAD = 16
MIB = 1024 * 1024


def normalize(wide):
    return wide * lax.rsqrt(jnp.sum(wide * wide, axis=-1, keepdims=True) + EPS)


def pack_kernel(owner_ref, local_ref, queries_ref, cent_ref, out_ref, count_ref, req_ref):
    peers = out_ref.shape[0]
    q_dev, per_query = owner_ref.shape
    qrows = queries_ref.shape[0] * queries_ref.shape[1]
    dim = queries_ref.shape[2]
    half = cent_ref.shape[0] // lax.axis_size("query")
    core = lax.axis_index("query")

    def clear(i, carry):
        count_ref[i] = 0
        return carry

    lax.fori_loop(0, peers, clear, 0)
    row = lax.broadcasted_iota(jnp.int32, req_ref.shape, 0)
    lane = lax.broadcasted_iota(jnp.int32, req_ref.shape, 1)
    req = jnp.full(req_ref.shape, -1, jnp.int32)
    for q in range(q_dev):
        for k in range(per_query):
            owner = owner_ref[q, k]
            slot = count_ref[owner]
            count_ref[owner] = slot + 1
            here = row == owner
            req = jnp.where(here & (lane == slot), local_ref[q, k], req)
            req = jnp.where(here & (lane == slot + dim // 2), q * per_query + k, req)
    req_ref[...] = req.astype(jnp.float32)
    qnorm = normalize(queries_ref[...].reshape(qrows, dim).astype(jnp.float32)).astype(jnp.bfloat16)
    cent = cent_ref[pl.ds(pl.multiple_of(core * half, 16), half), :]

    def send(d, carry):
        out_ref[d, :qrows, :] = qnorm
        out_ref[d, qrows : qrows + half, :] = cent
        out_ref[d, qrows + half :, :] = jnp.broadcast_to(req_ref[pl.ds(d, 1), :], (PAD, dim)).astype(
            jnp.bfloat16
        )
        return carry

    lax.fori_loop(0, peers, send, 0, unroll=peers <= 16)


def score_kernel(
    slots,
    q_dev,
    per_query,
    qtok,
    req_ref,
    length_ref,
    recv_ref,
    other_ref,
    codes_ref,
    resid_ref,
    out_ref,
    table_ref,
    dec_ref,
    cent_ref,
):
    peers, half, dim = other_ref.shape
    qrows = q_dev * qtok
    seq = codes_ref.shape[0]
    shard = 2 * half
    core = lax.axis_index("query")

    def place(h, carry):
        cols = pl.ds(pl.multiple_of(h * dim, dim), dim)
        table_ref[:half, cols] = recv_ref[h, qrows : qrows + half, :]
        table_ref[half:, cols] = other_ref[h]
        return carry

    lax.fori_loop(0, peers, place, 0, unroll=peers <= 16)
    lane = lax.broadcasted_iota(jnp.int32, (seq, dim), 1)
    token = lax.broadcasted_iota(jnp.int32, (seq, dim), 0)
    row8 = lax.broadcasted_iota(jnp.int32, (2 * q_dev, dim), 0)
    lane8 = lax.broadcasted_iota(jnp.int32, (2 * q_dev, dim), 1)
    lane1 = lax.broadcasted_iota(jnp.int32, (1, dim), 1)

    def block(b, carry):
        hot, high = [], []
        for s in range(slots):
            p = jnp.maximum(req_ref[b, s], 0)
            code = jnp.take_along_axis(codes_ref[...], jnp.full((seq, dim), p, jnp.int32), axis=1)
            low = (code % shard) ^ (core * half)
            high.append(code // shard)
            hot.append(
                jnp.concatenate([low == lane + i * dim for i in range(shard // dim)], axis=1)
                .astype(jnp.float32)
                .astype(jnp.bfloat16)
            )
        hot = jnp.concatenate(hot, axis=0)
        high = jnp.concatenate(high, axis=0)

        def pick(h, cent):
            cols = pl.ds(pl.multiple_of(2 * h * dim, 2 * dim), 2 * dim)
            rows = jnp.dot(hot, table_ref[:, cols], preferred_element_type=jnp.float32)
            cent = jnp.where(high == 2 * h, rows[:, :dim], cent)
            return jnp.where(high == 2 * h + 1, rows[:, dim:], cent)

        cent = lax.fori_loop(
            0, peers // 2, pick, jnp.zeros((slots * seq, dim), jnp.float32), unroll=peers <= 16
        )
        cent_ref[...] = cent.astype(jnp.bfloat16)
        for s in range(slots):
            p = jnp.maximum(req_ref[b, s], 0)
            v = cent[s * seq : (s + 1) * seq] + resid_ref[p].astype(jnp.float32)
            dec_ref[s * seq : (s + 1) * seq, :] = normalize(v).astype(jnp.bfloat16)
        query = recv_ref[b, :qrows, :]
        nt = (((1,), (1,)), ((), ()))
        exact = lax.dot_general(dec_ref[...], query, nt, preferred_element_type=jnp.float32)
        approx = lax.dot_general(cent_ref[...], query, nt, preferred_element_type=jnp.float32)
        total = jnp.zeros((2 * q_dev, dim), jnp.float32)
        for s in range(slots):
            p = jnp.maximum(req_ref[b, s], 0)
            c = req_ref[b, s + dim // 2]
            q, k = c // per_query, c % per_query
            live = token < length_ref[p]
            mine = lane1 // qtok == q
            for off, sims in ((0, exact), (q_dev, approx)):
                best = jnp.max(
                    jnp.where(live, sims[s * seq : (s + 1) * seq], -1000000000.0), axis=0, keepdims=True
                )
                score = jnp.sum(jnp.where(mine, best, 0.0), axis=1, keepdims=True)
                total += jnp.where((row8 == q + off) & (lane8 == k) & (c >= 0), score, 0.0)
        out_ref[b] = total
        return carry

    lax.fori_loop(0, peers, block, 0)


def body(queries, cand_owner, cand_local, centroids, passage_codes, residuals, passage_lengths):
    peers = lax.axis_size("index")
    cores = lax.axis_size("query")
    q_dev, per_query = cand_owner.shape
    count = q_dev * per_query
    slots = max(2, (2 * count + peers - 1) // peers)
    seq, dim = residuals.shape[1:]
    qtok = queries.shape[1]
    qrows = q_dev * qtok
    half = centroids.shape[0] // cores
    rows = qrows + half + PAD
    vmem = pl.BlockSpec(memory_space=pltpu.VMEM)
    smem = pl.BlockSpec(memory_space=pltpu.SMEM)
    scratch = 2 * peers * rows * dim // MIB
    params = pltpu.CompilerParams(vmem_limit_bytes=(8 + 2 * scratch) * MIB)
    packed = pl.pallas_call(
        pack_kernel,
        out_shape=jax.ShapeDtypeStruct((peers, rows, dim), jnp.bfloat16),
        in_specs=[smem, smem, vmem, vmem],
        out_specs=vmem,
        scratch_shapes=[pltpu.SMEM((peers,), jnp.int32), pltpu.VMEM((peers, dim), jnp.float32)],
        compiler_params=params,
    )(cand_owner, cand_local, queries, centroids)
    recv = lax.all_to_all(packed, "index", split_axis=0, concat_axis=0, tiled=True)
    other = lax.ppermute(recv[:, qrows : qrows + half, :], "query", [(0, 1), (1, 0)])
    requests = recv[:, qrows + half, :].astype(jnp.int32)
    scores = pl.pallas_call(
        functools.partial(score_kernel, slots, q_dev, per_query, qtok),
        out_shape=jax.ShapeDtypeStruct((peers, 2 * q_dev, dim), jnp.float32),
        in_specs=[smem, smem, vmem, vmem, vmem, vmem],
        out_specs=vmem,
        scratch_shapes=[
            pltpu.VMEM((cores * half, peers * dim), jnp.bfloat16),
            pltpu.VMEM((slots * seq, dim), jnp.bfloat16),
            pltpu.VMEM((slots * seq, dim), jnp.bfloat16),
        ],
        compiler_params=params,
    )(requests, passage_lengths, recv, other, passage_codes.T, residuals)
    back = lax.all_to_all(scores, "index", split_axis=0, concat_axis=0, tiled=True)
    result = jnp.sum(back[:, :, :per_query], axis=0)
    return result[:q_dev], result[q_dev:]


def solution(mesh):
    in_specs = (
        P(("group", "index", "query"), None, None),
        P(("group", "index", "query"), None),
        P(("group", "index", "query"), None),
        P("index", None),
        P("index", None),
        P("index", None, None),
        P("index"),
    )
    out_specs = (P(("group", "index", "query"), None), P(("group", "index", "query"), None))
    return jax.shard_map(body, mesh=mesh, in_specs=in_specs, out_specs=out_specs, check_vma=False)
```

```python
import functools

import jax
import jax.numpy as jnp
from jax import lax
from jax.experimental import pallas as pl
from jax.experimental.pallas import tpu as pltpu
from jax.sharding import PartitionSpec as P

EPS = 1e-06
PAD = 16
MIB = 1024 * 1024


def normalize(wide):
    return wide * lax.rsqrt(jnp.sum(wide * wide, axis=-1, keepdims=True) + EPS)


def pack_kernel(
    owner_hbm, local_hbm, queries_hbm, out_ref, count_ref, req_ref, owner_ref, local_ref, queries_ref, sems
):
    copies = [
        pltpu.make_async_copy(src, dst, sems.at[i])
        for i, (src, dst) in enumerate(
            ((owner_hbm, owner_ref), (local_hbm, local_ref), (queries_hbm, queries_ref))
        )
    ]
    for copy in copies:
        copy.start()
    for copy in copies:
        copy.wait()
    peers = out_ref.shape[0]
    q_dev, per_query = owner_ref.shape
    qrows = queries_ref.shape[0] * queries_ref.shape[1]
    dim = queries_ref.shape[2]

    def clear(i, carry):
        count_ref[i] = 0
        return carry

    lax.fori_loop(0, peers, clear, 0)
    row = lax.broadcasted_iota(jnp.int32, req_ref.shape, 0)
    lane = lax.broadcasted_iota(jnp.int32, req_ref.shape, 1)
    req = jnp.full(req_ref.shape, -1, jnp.int32)
    for q in range(q_dev):
        for k in range(per_query):
            owner = owner_ref[q, k]
            slot = count_ref[owner]
            count_ref[owner] = slot + 1
            here = row == owner
            req = jnp.where(here & (lane == slot), local_ref[q, k], req)
            req = jnp.where(here & (lane == slot + dim // 2), q * per_query + k, req)
    req_ref[...] = req.astype(jnp.float32)
    qnorm = normalize(queries_ref[...].reshape(qrows, dim).astype(jnp.float32)).astype(jnp.bfloat16)

    def send(d, carry):
        out_ref[d, :qrows, :] = qnorm
        out_ref[d, qrows:, :] = jnp.broadcast_to(req_ref[pl.ds(d, 1), :], (PAD, dim)).astype(
            jnp.bfloat16
        )
        return carry

    lax.fori_loop(0, peers, send, 0, unroll=peers <= 16)


def score_kernel(
    slots,
    q_dev,
    per_query,
    qtok,
    req_ref,
    length_ref,
    recv_ref,
    mine_ref,
    other_ref,
    codes_ref,
    resid_ref,
    out_ref,
    table_ref,
    dec_ref,
    cent_ref,
):
    peers, half, dim = other_ref.shape
    qrows = q_dev * qtok
    seq = codes_ref.shape[0]
    shard = 2 * half
    me = lax.axis_index("index")
    core = lax.axis_index("query")

    def place(h, carry):
        cols = pl.ds(pl.multiple_of((h ^ me) * dim, dim), dim)
        table_ref[:half, cols] = mine_ref[h]
        table_ref[half:, cols] = other_ref[h]
        return carry

    lax.fori_loop(0, peers, place, 0, unroll=peers <= 16)
    lane = lax.broadcasted_iota(jnp.int32, (seq, dim), 1)
    token = lax.broadcasted_iota(jnp.int32, (seq, dim), 0)
    row8 = lax.broadcasted_iota(jnp.int32, (2 * q_dev, dim), 0)
    lane8 = lax.broadcasted_iota(jnp.int32, (2 * q_dev, dim), 1)
    lane1 = lax.broadcasted_iota(jnp.int32, (1, dim), 1)

    def block(b, carry):
        hot, high = [], []
        for s in range(slots):
            p = jnp.maximum(req_ref[b, s], 0)
            code = jnp.take_along_axis(codes_ref[...], jnp.full((seq, dim), p, jnp.int32), axis=1)
            low = (code % shard) ^ (core * half)
            high.append(code // shard)
            hot.append(
                jnp.concatenate([low == lane + i * dim for i in range(shard // dim)], axis=1)
                .astype(jnp.float32)
                .astype(jnp.bfloat16)
            )
        hot = jnp.concatenate(hot, axis=0)
        high = jnp.concatenate(high, axis=0)

        def pick(h, cent):
            cols = pl.ds(pl.multiple_of(2 * h * dim, 2 * dim), 2 * dim)
            rows = jnp.dot(hot, table_ref[:, cols], preferred_element_type=jnp.float32)
            cent = jnp.where(high == 2 * h, rows[:, :dim], cent)
            return jnp.where(high == 2 * h + 1, rows[:, dim:], cent)

        cent = lax.fori_loop(
            0, peers // 2, pick, jnp.zeros((slots * seq, dim), jnp.float32), unroll=peers <= 16
        )
        cent_ref[...] = cent.astype(jnp.bfloat16)
        for s in range(slots):
            p = jnp.maximum(req_ref[b, s], 0)
            v = cent[s * seq : (s + 1) * seq] + resid_ref[p].astype(jnp.float32)
            dec_ref[s * seq : (s + 1) * seq, :] = normalize(v).astype(jnp.bfloat16)
        query = recv_ref[b, :qrows, :]
        nt = (((1,), (1,)), ((), ()))
        exact = lax.dot_general(dec_ref[...], query, nt, preferred_element_type=jnp.float32)
        approx = lax.dot_general(cent_ref[...], query, nt, preferred_element_type=jnp.float32)
        total = jnp.zeros((2 * q_dev, dim), jnp.float32)
        for s in range(slots):
            p = jnp.maximum(req_ref[b, s], 0)
            c = req_ref[b, s + dim // 2]
            q, k = c // per_query, c % per_query
            live = token < length_ref[p]
            mine = lane1 // qtok == q
            for off, sims in ((0, exact), (q_dev, approx)):
                best = jnp.max(
                    jnp.where(live, sims[s * seq : (s + 1) * seq], -1000000000.0), axis=0, keepdims=True
                )
                score = jnp.sum(jnp.where(mine, best, 0.0), axis=1, keepdims=True)
                total += jnp.where((row8 == q + off) & (lane8 == k) & (c >= 0), score, 0.0)
        out_ref[b] = total
        return carry

    lax.fori_loop(0, peers, block, 0)


def gather_table(centroids):
    peers, cores = lax.axis_size("index"), lax.axis_size("query")
    half = centroids.shape[0] // cores
    core = lax.axis_index("query")
    swap = lambda x, t: lax.ppermute(x, "index", [(i, i ^ t) for i in range(peers)])
    both = jnp.stack([centroids, swap(centroids, 1)])
    have = lax.dynamic_slice_in_dim(both, core * half, half, axis=1)
    while have.shape[0] < peers:
        step = have.shape[0]
        radix = min(4, peers // step)
        have = jnp.concatenate([have] + [swap(have, m * step) for m in range(1, radix)], axis=0)
    return have


def body(queries, cand_owner, cand_local, centroids, passage_codes, residuals, passage_lengths):
    peers = lax.axis_size("index")
    cores = lax.axis_size("query")
    q_dev, per_query = cand_owner.shape
    count = q_dev * per_query
    slots = max(2, (2 * count + peers - 1) // peers)
    seq, dim = residuals.shape[1:]
    qtok = queries.shape[1]
    qrows = q_dev * qtok
    half = centroids.shape[0] // cores
    rows = qrows + PAD
    vmem = pl.BlockSpec(memory_space=pltpu.VMEM)
    smem = pl.BlockSpec(memory_space=pltpu.SMEM)
    hbm = pl.BlockSpec(memory_space=pltpu.HBM)
    pack_mib = 2 * peers * rows * dim * 2 // MIB
    packed = pl.pallas_call(
        pack_kernel,
        out_shape=jax.ShapeDtypeStruct((peers, rows, dim), jnp.bfloat16),
        in_specs=[hbm, hbm, hbm],
        out_specs=vmem,
        scratch_shapes=[
            pltpu.SMEM((peers,), jnp.int32),
            pltpu.VMEM((peers, dim), jnp.float32),
            pltpu.SMEM(cand_owner.shape, jnp.int32),
            pltpu.SMEM(cand_local.shape, jnp.int32),
            pltpu.VMEM(queries.shape, queries.dtype),
            pltpu.SemaphoreType.DMA((3,)),
        ],
        compiler_params=pltpu.CompilerParams(vmem_limit_bytes=(4 + pack_mib) * MIB),
    )(cand_owner, cand_local, queries)
    recv = lax.all_to_all(packed, "index", split_axis=0, concat_axis=0, tiled=True)
    mine = gather_table(centroids)
    other = lax.ppermute(mine, "query", [(0, 1), (1, 0)])
    requests = recv[:, qrows, :].astype(jnp.int32)
    table_mib = 2 * peers * half * dim * 2 // MIB
    scores = pl.pallas_call(
        functools.partial(score_kernel, slots, q_dev, per_query, qtok),
        out_shape=jax.ShapeDtypeStruct((peers, 2 * q_dev, dim), jnp.float32),
        in_specs=[smem, smem, vmem, vmem, vmem, vmem, vmem],
        out_specs=vmem,
        scratch_shapes=[
            pltpu.VMEM((cores * half, peers * dim), jnp.bfloat16),
            pltpu.VMEM((slots * seq, dim), jnp.bfloat16),
            pltpu.VMEM((slots * seq, dim), jnp.bfloat16),
        ],
        compiler_params=pltpu.CompilerParams(vmem_limit_bytes=(8 + 2 * table_mib) * MIB),
    )(requests, passage_lengths, recv, mine, other, passage_codes.T, residuals)
    back = lax.all_to_all(scores, "index", split_axis=0, concat_axis=0, tiled=True)
    result = jnp.sum(back[:, :, :per_query], axis=0)
    return result[:q_dev], result[q_dev:]


def solution(mesh):
    in_specs = (
        P(("group", "index", "query"), None, None),
        P(("group", "index", "query"), None),
        P(("group", "index", "query"), None),
        P("index", None),
        P("index", None),
        P("index", None, None),
        P("index"),
    )
    out_specs = (P(("group", "index", "query"), None), P(("group", "index", "query"), None))
    return jax.shard_map(body, mesh=mesh, in_specs=in_specs, out_specs=out_specs, check_vma=False)
```

```python
import functools

import jax
import jax.numpy as jnp
from jax import lax
from jax.experimental import pallas as pl
from jax.experimental.pallas import tpu as pltpu
from jax.sharding import PartitionSpec as P

EPS = 1e-06
PAD = 16
MIB = 1024 * 1024


def normalize(wide):
    return wide * lax.rsqrt(jnp.sum(wide * wide, axis=-1, keepdims=True) + EPS)


def pack_kernel(
    owner_hbm,
    local_hbm,
    queries_hbm,
    cent_hbm,
    codes_hbm,
    resid_hbm,
    length_hbm,
    out_ref,
    codes_out,
    resid_out,
    length_out,
    count_ref,
    req_ref,
    owner_ref,
    local_ref,
    queries_ref,
    cent_ref,
    sems,
):
    copies = out_ref.shape[0]
    peers = count_ref.shape[0]
    q_dev, per_query = owner_ref.shape
    qrows = queries_ref.shape[0] * queries_ref.shape[1]
    half, dim = cent_ref.shape
    core = lax.axis_index("query")
    cent_half = cent_hbm.at[pl.ds(pl.multiple_of(core * half, 16), half)]
    moves = [
        pltpu.make_async_copy(src, dst, sems.at[i])
        for i, (src, dst) in enumerate(
            (
                (owner_hbm, owner_ref),
                (local_hbm, local_ref),
                (queries_hbm, queries_ref),
                (cent_half, cent_ref),
                (codes_hbm, codes_out),
                (length_hbm, length_out),
                (resid_hbm, resid_out),
            )
        )
    ]
    for move in moves:
        move.start()

    def clear(i, carry):
        count_ref[i] = 0
        return carry

    lax.fori_loop(0, peers, clear, 0)
    for move in moves[:4]:
        move.wait()
    row = lax.broadcasted_iota(jnp.int32, req_ref.shape, 0)
    lane = lax.broadcasted_iota(jnp.int32, req_ref.shape, 1)
    req = jnp.full(req_ref.shape, -1, jnp.int32)
    for q in range(q_dev):
        for k in range(per_query):
            owner = owner_ref[q, k]
            slot = count_ref[owner]
            count_ref[owner] = slot + 1
            here = row == owner
            req = jnp.where(here & (lane == slot), local_ref[q, k], req)
            req = jnp.where(here & (lane == slot + dim // 2), q * per_query + k, req)
    req_ref[...] = req.astype(jnp.float32)
    qnorm = normalize(queries_ref[...].reshape(qrows, dim).astype(jnp.float32)).astype(jnp.bfloat16)

    def send(d, carry):
        out_ref[d, :qrows, :] = qnorm
        out_ref[d, qrows : qrows + half, :] = cent_ref[...]
        asked = req_ref[pl.ds(d, PAD), :]
        out_ref[d, qrows + half :, :] = asked.astype(jnp.bfloat16)
        return carry

    lax.fori_loop(0, copies, send, 0)
    for move in moves[4:]:
        move.wait()


def score_kernel(slots, q_dev, per_query, qtok, order, req_ref, length_ref, *refs):
    *parts, other_ref, codes_ref, resid_ref, out_ref, query_ref, table_ref, dec_ref, cent_ref = refs
    peers, half, dim = other_ref.shape
    qrows = q_dev * qtok
    seq = codes_ref.shape[0]
    shard = 2 * half
    me = lax.axis_index("index")
    core = lax.axis_index("query")

    def place(t, part, swapped):
        peer = me ^ order[t] if order else t
        cols = pl.ds(pl.multiple_of(peer * dim, dim), dim)
        table_ref[:half, cols] = part[qrows : qrows + half, :]
        table_ref[half:, cols] = swapped[...]
        query_ref[t] = part[:qrows, :]

    def place_loop(t, carry):
        place(t, parts[0].at[t], other_ref.at[t])
        return carry

    if order:
        for t in range(peers):
            place(t, parts[t], other_ref.at[t])
    else:
        lax.fori_loop(0, peers, place_loop, 0)
    lane = lax.broadcasted_iota(jnp.int32, (seq, dim), 1)
    token = lax.broadcasted_iota(jnp.int32, (seq, dim), 0)
    row8 = lax.broadcasted_iota(jnp.int32, (2 * q_dev, dim), 0)
    lane8 = lax.broadcasted_iota(jnp.int32, (2 * q_dev, dim), 1)
    lane1 = lax.broadcasted_iota(jnp.int32, (1, dim), 1)

    def block(b, carry):
        hot, high = [], []
        for s in range(slots):
            p = jnp.maximum(req_ref[b, s], 0)
            code = jnp.take_along_axis(codes_ref[...], jnp.full((seq, dim), p, jnp.int32), axis=1)
            low = (code % shard) ^ (core * half)
            high.append(code // shard)
            hot.append(
                jnp.concatenate([low == lane + i * dim for i in range(shard // dim)], axis=1)
                .astype(jnp.float32)
                .astype(jnp.bfloat16)
            )
        hot = jnp.concatenate(hot, axis=0)
        high = jnp.concatenate(high, axis=0)

        def pick(h, cent):
            cols = pl.ds(pl.multiple_of(2 * h * dim, 2 * dim), 2 * dim)
            rows = jnp.dot(hot, table_ref[:, cols], preferred_element_type=jnp.float32)
            cent = jnp.where(high == 2 * h, rows[:, :dim], cent)
            return jnp.where(high == 2 * h + 1, rows[:, dim:], cent)

        cent = lax.fori_loop(
            0, peers // 2, pick, jnp.zeros((slots * seq, dim), jnp.float32), unroll=peers <= 16
        )
        cent_ref[...] = cent.astype(jnp.bfloat16)
        for s in range(slots):
            p = jnp.maximum(req_ref[b, s], 0)
            v = cent[s * seq : (s + 1) * seq] + resid_ref[p].astype(jnp.float32)
            dec_ref[s * seq : (s + 1) * seq, :] = normalize(v).astype(jnp.bfloat16)
        query = query_ref[b]
        nt = (((1,), (1,)), ((), ()))
        exact = lax.dot_general(dec_ref[...], query, nt, preferred_element_type=jnp.float32)
        approx = lax.dot_general(cent_ref[...], query, nt, preferred_element_type=jnp.float32)
        total = jnp.zeros((2 * q_dev, dim), jnp.float32)
        for s in range(slots):
            p = jnp.maximum(req_ref[b, s], 0)
            c = req_ref[b, s + dim // 2]
            q, k = c // per_query, c % per_query
            live = token < length_ref[p]
            mine = lane1 // qtok == q
            for off, sims in ((0, exact), (q_dev, approx)):
                best = jnp.max(
                    jnp.where(live, sims[s * seq : (s + 1) * seq], -1000000000.0), axis=0, keepdims=True
                )
                score = jnp.sum(jnp.where(mine, best, 0.0), axis=1, keepdims=True)
                total += jnp.where((row8 == q + off) & (lane8 == k) & (c >= 0), score, 0.0)
        out_ref[me ^ (peers - 1 - b) if order else b] = total
        return carry

    lax.fori_loop(0, peers, block, 0)


def body(queries, cand_owner, cand_local, centroids, passage_codes, residuals, passage_lengths):
    peers = lax.axis_size("index")
    cores = lax.axis_size("query")
    q_dev, per_query = cand_owner.shape
    count = q_dev * per_query
    slots = max(2, (2 * count + peers - 1) // peers)
    seq, dim = residuals.shape[1:]
    qtok = queries.shape[1]
    qrows = q_dev * qtok
    half = centroids.shape[0] // cores
    rows = qrows + half + PAD
    order = tuple(range(peers - 1, -1, -1)) if peers <= PAD and peers & (peers - 1) == 0 else ()
    vmem = pl.BlockSpec(memory_space=pltpu.VMEM)
    smem = pl.BlockSpec(memory_space=pltpu.SMEM)
    hbm = pl.BlockSpec(memory_space=pltpu.HBM)
    copies = 1 if order else peers
    pack_mib = 2 * copies * rows * dim * 2 // MIB
    held = [passage_codes.T, residuals, passage_lengths]
    inputs = [cand_owner, cand_local, queries, centroids] + held
    packed, *held = pl.pallas_call(
        pack_kernel,
        out_shape=[jax.ShapeDtypeStruct((copies, rows, dim), jnp.bfloat16)]
        + [jax.ShapeDtypeStruct(x.shape, x.dtype) for x in held],
        in_specs=[hbm] * 7,
        out_specs=[vmem] * 4,
        scratch_shapes=[
            pltpu.SMEM((peers,), jnp.int32),
            pltpu.VMEM((peers + PAD, dim), jnp.float32),
            pltpu.SMEM(cand_owner.shape, jnp.int32),
            pltpu.SMEM(cand_local.shape, jnp.int32),
            pltpu.VMEM(queries.shape, queries.dtype),
            pltpu.VMEM((half, dim), centroids.dtype),
            pltpu.SemaphoreType.DMA((7,)),
        ],
        compiler_params=pltpu.CompilerParams(vmem_limit_bytes=(8 + pack_mib) * MIB),
    )(*(pltpu.with_memory_space_constraint(x, pltpu.HBM) for x in inputs))
    codes, resid, lengths = held
    if order:
        parts = [
            lax.ppermute(packed[0], "index", [(i, i ^ t) for i in range(peers)]) if t else packed[0]
            for t in order
        ]
        mine = jnp.stack([part[qrows : qrows + half] for part in parts])
        asked = jnp.stack([part[qrows + half :] for part in parts])
        asked = lax.dynamic_index_in_dim(asked, lax.axis_index("index"), 1, keepdims=False)
    else:
        parts = [lax.all_to_all(packed, "index", split_axis=0, concat_axis=0, tiled=True)]
        mine = parts[0][:, qrows : qrows + half]
        asked = parts[0][:, qrows + half]
    other = lax.ppermute(mine, "query", [(0, 1), (1, 0)])
    table_mib = 2 * peers * half * dim * 2 // MIB
    scores = pl.pallas_call(
        functools.partial(score_kernel, slots, q_dev, per_query, qtok, order),
        out_shape=jax.ShapeDtypeStruct((peers, 2 * q_dev, dim), jnp.float32),
        in_specs=[smem, smem] + [vmem] * (len(parts) + 3),
        out_specs=vmem,
        scratch_shapes=[
            pltpu.VMEM((peers, qrows, dim), jnp.bfloat16),
            pltpu.VMEM((cores * half, peers * dim), jnp.bfloat16),
            pltpu.VMEM((slots * seq, dim), jnp.bfloat16),
            pltpu.VMEM((slots * seq, dim), jnp.bfloat16),
        ],
        compiler_params=pltpu.CompilerParams(vmem_limit_bytes=(8 + 2 * table_mib) * MIB),
    )(asked.astype(jnp.int32), lengths, *parts, other, codes, resid)
    back = lax.all_to_all(scores, "index", split_axis=0, concat_axis=0, tiled=True)
    result = jnp.sum(back[:, :, :per_query], axis=0)
    return result[:q_dev], result[q_dev:]


def solution(mesh):
    in_specs = (
        P(("group", "index", "query"), None, None),
        P(("group", "index", "query"), None),
        P(("group", "index", "query"), None),
        P("index", None),
        P("index", None),
        P("index", None, None),
        P("index"),
    )
    out_specs = (P(("group", "index", "query"), None), P(("group", "index", "query"), None))
    return jax.shard_map(body, mesh=mesh, in_specs=in_specs, out_specs=out_specs, check_vma=False)
```

```python
import functools

import jax
import jax.numpy as jnp
from jax import lax
from jax.experimental import pallas as pl
from jax.experimental.pallas import tpu as pltpu
from jax.sharding import PartitionSpec as P

EPS = 1e-06
PAD = 16
UNIT = 32
GROUP = 16
MIB = 1024 * 1024


def normalize(wide):
    return wide * lax.rsqrt(jnp.sum(wide * wide, axis=-1, keepdims=True) + EPS)


def pack_kernel(
    owner_hbm,
    local_hbm,
    queries_hbm,
    cent_hbm,
    codes_hbm,
    resid_hbm,
    length_hbm,
    out_ref,
    codes_out,
    resid_out,
    length_out,
    count_ref,
    req_ref,
    owner_ref,
    local_ref,
    queries_ref,
    cent_ref,
    sems,
):
    copies = out_ref.shape[0]
    peers = count_ref.shape[0]
    q_dev, per_query = owner_ref.shape
    qrows = queries_ref.shape[0] * queries_ref.shape[1]
    half, dim = cent_ref.shape
    core = lax.axis_index("query")
    cent_half = cent_hbm.at[pl.ds(pl.multiple_of(core * half, 16), half)]
    moves = [
        pltpu.make_async_copy(src, dst, sems.at[i])
        for i, (src, dst) in enumerate(
            (
                (owner_hbm, owner_ref),
                (local_hbm, local_ref),
                (queries_hbm, queries_ref),
                (cent_half, cent_ref),
                (codes_hbm, codes_out),
                (length_hbm, length_out),
                (resid_hbm, resid_out),
            )
        )
    ]
    for move in moves:
        move.start()

    def clear(i, carry):
        count_ref[i] = 0
        return carry

    lax.fori_loop(0, peers, clear, 0)
    for move in moves[:4]:
        move.wait()
    row = lax.broadcasted_iota(jnp.int32, req_ref.shape, 0)
    lane = lax.broadcasted_iota(jnp.int32, req_ref.shape, 1)
    req = jnp.full(req_ref.shape, -1, jnp.int32)
    for q in range(q_dev):
        for k in range(per_query):
            owner = owner_ref[q, k]
            slot = count_ref[owner]
            count_ref[owner] = slot + 1
            here = row == owner
            req = jnp.where(here & (lane == slot), local_ref[q, k], req)
            req = jnp.where(here & (lane == slot + dim // 2), q * per_query + k, req)
    req_ref[...] = req.astype(jnp.float32)
    qnorm = normalize(queries_ref[...].reshape(qrows, dim).astype(jnp.float32)).astype(jnp.bfloat16)

    def send(d, carry):
        out_ref[d, :qrows, :] = qnorm
        out_ref[d, qrows : qrows + half, :] = cent_ref[...]
        asked = req_ref[pl.ds(d, PAD), :]
        out_ref[d, qrows + half :, :] = asked.astype(jnp.bfloat16)
        return carry

    lax.fori_loop(0, copies, send, 0)
    for move in moves[4:]:
        move.wait()


def score_kernel(slots, q_dev, per_query, qtok, order, req_ref, length_ref, codes_any, *refs):
    (*parts, other_ref, resid_ref, out_ref) = refs[:-10]
    query_ref, table_ref, rows_ref, more_ref, best_ref, near_ref, cand_ref, units_ref, codes_ref, sem = refs[-10:]
    peers, half, dim = other_ref.shape
    qrows = q_dev * qtok
    passages, seq = resid_ref.shape[:2]
    pieces = seq // UNIT
    shard = 2 * half
    total = peers * slots
    me = lax.axis_index("index")
    core = lax.axis_index("query")

    bring = pltpu.make_async_copy(codes_any, codes_ref, sem)
    bring.start()
    best_ref[...] = jnp.full(best_ref.shape, -1000000000.0, jnp.float32)
    near_ref[...] = jnp.full(near_ref.shape, -1000000000.0, jnp.float32)

    piece_bits = (pieces - 1).bit_length()
    pass_bits = (passages - 1).bit_length()
    slot_bits = total.bit_length()
    cand_bits = (per_query - 1).bit_length()
    slot_at = piece_bits + pass_bits
    head_at = slot_at + slot_bits

    def field(word, at, bits):
        return lax.shift_right_logical(word, at) & ((1 << bits) - 1)

    def listing(b, n):
        for s in range(slots):
            p = req_ref[b, s]
            c = req_ref[b, s + dim // 2]
            slot = b * slots + s
            cand_ref[pl.ds(slot, 1), :] = jnp.full((1, dim), c, jnp.int32)
            length = jnp.where(p >= 0, length_ref[jnp.maximum(p, 0)], 0)
            head = b * q_dev + lax.shift_right_logical(c, cand_bits)
            word = (head << head_at) + (slot << slot_at) + (p << piece_bits)
            for u in range(pieces):
                units_ref[n] = word + u
                n = n + jnp.where(length > u * UNIT, 1, 0)
        return n

    count = lax.fori_loop(0, peers, listing, 0)
    for u in range(3 * GROUP):
        units_ref[count + u] = total << slot_at

    def place(t, part, swapped):
        peer = me ^ order[t] if order else t
        first = pl.multiple_of(peer * shard + core * half, 8)
        second = pl.multiple_of(peer * shard + half - core * half, 8)
        table_ref[pl.ds(first, half), :] = part[qrows : qrows + half, :].astype(jnp.float32)
        table_ref[pl.ds(second, half), :] = swapped[...].astype(jnp.float32)
        query_ref[pl.ds(pl.multiple_of(t * qrows, 16), qrows), :] = part[:qrows, :]

    def place_loop(t, carry):
        place(t, parts[0].at[t], other_ref.at[t])
        return carry

    if order:
        for t in range(peers):
            place(t, parts[t], other_ref.at[t])
    else:
        lax.fori_loop(0, peers, place_loop, 0)

    token = lax.broadcasted_iota(jnp.int32, (UNIT, qtok), 0)
    nt = (((1,), (1,)), ((), ()))

    def fetch(g, j, rows):
        word = units_ref[g * GROUP + j]
        base = field(word, 0, piece_bits) * (UNIT * passages) + field(word, piece_bits, pass_bits)
        for t in range(UNIT):
            rows[j * UNIT + t : j * UNIT + t + 1, :] = table_ref[pl.ds(codes_ref[base + t * passages], 1), :]

    def compare(g, j, rows):
        word = units_ref[g * GROUP + j]
        piece = field(word, 0, piece_bits)
        p = field(word, piece_bits, pass_bits)
        row = piece * (total + 8) + field(word, slot_at, slot_bits)
        head = lax.shift_right_logical(word, head_at)
        resid = resid_ref[p, pl.ds(pl.multiple_of(piece * UNIT, UNIT), UNIT), :]
        query = query_ref[pl.ds(pl.multiple_of(head * qtok, qtok), qtok), :]
        left = length_ref[p] - piece * UNIT
        cent = rows[j * UNIT : (j + 1) * UNIT, :]
        v = cent + resid.astype(jnp.float32)
        both = jnp.concatenate([normalize(v).astype(jnp.bfloat16), cent.astype(jnp.bfloat16)], axis=0)
        sims = lax.dot_general(both, query, nt, preferred_element_type=jnp.float32)
        tops = [
            jnp.max(jnp.where(token < left, sims[o : o + UNIT], -1000000000.0), axis=0, keepdims=True)
            for o in (0, UNIT)
        ]
        return row, tops

    def step(g, now, later):
        found = []
        for j in range(GROUP):
            found.append(compare(g, j, now))
            fetch(g + 1, j, later)
        for row, (exact, approx) in found:
            best_ref[pl.ds(row, 1), :] = exact
            near_ref[pl.ds(row, 1), :] = approx

    def pair(i, carry):
        step(2 * i, rows_ref, more_ref)
        step(2 * i + 1, more_ref, rows_ref)
        return carry

    bring.wait()
    for j in range(GROUP):
        fetch(0, j, rows_ref)
    lax.fori_loop(0, (count + 2 * GROUP - 1) // (2 * GROUP), pair, 0)

    def score(ref):
        best = ref[:total, :]
        for u in range(1, pieces):
            best = jnp.maximum(best, ref[u * (total + 8) : u * (total + 8) + total, :])
        return jnp.sum(best, axis=1, keepdims=True)

    cand = cand_ref[...]
    lane = lax.broadcasted_iota(jnp.int32, (total, dim), 1)
    placed = jnp.where(lane == cand, score(best_ref), 0.0)
    placed += jnp.where(lane == cand + q_dev * per_query, score(near_ref), 0.0)
    placed = jnp.where(cand >= 0, placed, 0.0)
    placed = jnp.sum(placed.reshape(peers, slots, dim), axis=1)
    turned = [placed] + [pltpu.roll(placed, dim - r * per_query, 1) for r in range(1, 2 * q_dev)]
    for b in range(peers):
        to = me ^ order[b] if order else b
        for r in range(2 * q_dev):
            out_ref[to, r : r + 1, :] = turned[r][b : b + 1, :]


def body(queries, cand_owner, cand_local, centroids, passage_codes, residuals, passage_lengths):
    peers = lax.axis_size("index")
    cores = lax.axis_size("query")
    q_dev, per_query = cand_owner.shape
    count = q_dev * per_query
    slots = max(2, (2 * count + peers - 1) // peers)
    seq, dim = residuals.shape[1:]
    qtok = queries.shape[1]
    qrows = q_dev * qtok
    half = centroids.shape[0] // cores
    rows = qrows + half + PAD
    order = tuple(range(peers - 1, -1, -1)) if peers <= PAD and peers & (peers - 1) == 0 else ()
    vmem = pl.BlockSpec(memory_space=pltpu.VMEM)
    smem = pl.BlockSpec(memory_space=pltpu.SMEM)
    hbm = pl.BlockSpec(memory_space=pltpu.HBM)
    copies = 1 if order else peers
    pack_mib = 2 * copies * rows * dim * 2 // MIB
    held = [passage_codes.T.reshape(-1), residuals, passage_lengths]
    inputs = [cand_owner, cand_local, queries, centroids] + held
    packed, *held = pl.pallas_call(
        pack_kernel,
        out_shape=[jax.ShapeDtypeStruct((copies, rows, dim), jnp.bfloat16)]
        + [jax.ShapeDtypeStruct(x.shape, x.dtype) for x in held],
        in_specs=[hbm] * 7,
        out_specs=[vmem] * 4,
        scratch_shapes=[
            pltpu.SMEM((peers,), jnp.int32),
            pltpu.VMEM((peers + PAD, dim), jnp.float32),
            pltpu.SMEM(cand_owner.shape, jnp.int32),
            pltpu.SMEM(cand_local.shape, jnp.int32),
            pltpu.VMEM(queries.shape, queries.dtype),
            pltpu.VMEM((half, dim), centroids.dtype),
            pltpu.SemaphoreType.DMA((7,)),
        ],
        compiler_params=pltpu.CompilerParams(vmem_limit_bytes=(8 + pack_mib) * MIB),
    )(*(pltpu.with_memory_space_constraint(x, pltpu.HBM) for x in inputs))
    codes, resid, lengths = held
    if order:
        parts = [
            lax.ppermute(packed[0], "index", [(i, i ^ t) for i in range(peers)]) if t else packed[0]
            for t in order
        ]
        mine = jnp.stack([part[qrows : qrows + half] for part in parts])
        asked = jnp.stack([part[qrows + half :] for part in parts])
        asked = lax.dynamic_index_in_dim(asked, lax.axis_index("index"), 1, keepdims=False)
    else:
        parts = [lax.all_to_all(packed, "index", split_axis=0, concat_axis=0, tiled=True)]
        mine = parts[0][:, qrows : qrows + half]
        asked = parts[0][:, qrows + half]
    other = lax.ppermute(mine, "query", [(0, 1), (1, 0)])
    table_mib = 2 * peers * half * dim * 2 // MIB
    bests = (seq // UNIT) * (peers * slots + 8)
    scores = pl.pallas_call(
        functools.partial(score_kernel, slots, q_dev, per_query, qtok, order),
        out_shape=jax.ShapeDtypeStruct((peers, 2 * q_dev, dim), jnp.float32),
        in_specs=[smem, smem, pl.BlockSpec(memory_space=pl.ANY)] + [vmem] * (len(parts) + 2),
        out_specs=vmem,
        scratch_shapes=[
            pltpu.VMEM((peers * qrows, dim), jnp.bfloat16),
            pltpu.VMEM((peers * cores * half, dim), jnp.float32),
            pltpu.VMEM((GROUP * UNIT, dim), jnp.float32),
            pltpu.VMEM((GROUP * UNIT, dim), jnp.float32),
            pltpu.VMEM((bests, qtok), jnp.float32),
            pltpu.VMEM((bests, qtok), jnp.float32),
            pltpu.VMEM((peers * slots, dim), jnp.int32),
            pltpu.SMEM((peers * slots * (seq // UNIT) + 3 * GROUP,), jnp.int32),
            pltpu.SMEM(codes.shape, jnp.int32),
            pltpu.SemaphoreType.DMA,
        ],
        compiler_params=pltpu.CompilerParams(vmem_limit_bytes=(8 + 4 * table_mib) * MIB),
    )(asked.astype(jnp.int32), lengths, codes, *parts, other, resid)
    back = lax.all_to_all(scores, "index", split_axis=0, concat_axis=0, tiled=True)
    result = jnp.sum(back[:, :, :per_query], axis=0)
    return result[:q_dev], result[q_dev:]


def solution(mesh):
    in_specs = (
        P(("group", "index", "query"), None, None),
        P(("group", "index", "query"), None),
        P(("group", "index", "query"), None),
        P("index", None),
        P("index", None),
        P("index", None, None),
        P("index"),
    )
    out_specs = (P(("group", "index", "query"), None), P(("group", "index", "query"), None))
    return jax.shard_map(body, mesh=mesh, in_specs=in_specs, out_specs=out_specs, check_vma=False)
```

```python
import functools

import jax
import jax.numpy as jnp
from jax import lax
from jax.experimental import pallas as pl
from jax.experimental.pallas import tpu as pltpu
from jax.sharding import PartitionSpec as P

EPS = 1e-06
PAD = 16
UNIT = 32
GROUP = 32
FETCH = 8
MIB = 1024 * 1024


def normalize(wide):
    return wide * lax.rsqrt(jnp.sum(wide * wide, axis=-1, keepdims=True) + EPS)


def pack_kernel(
    owner_hbm,
    local_hbm,
    queries_hbm,
    cent_hbm,
    codes_hbm,
    resid_hbm,
    length_hbm,
    out_ref,
    codes_out,
    resid_out,
    length_out,
    count_ref,
    req_ref,
    owner_ref,
    local_ref,
    queries_ref,
    cent_ref,
    sems,
):
    copies = out_ref.shape[0]
    peers = count_ref.shape[0]
    q_dev, per_query = owner_ref.shape
    qrows = queries_ref.shape[0] * queries_ref.shape[1]
    half, dim = cent_ref.shape
    core = lax.axis_index("query")
    cent_half = cent_hbm.at[pl.ds(pl.multiple_of(core * half, 16), half)]
    moves = [
        pltpu.make_async_copy(src, dst, sems.at[i])
        for i, (src, dst) in enumerate(
            (
                (owner_hbm, owner_ref),
                (local_hbm, local_ref),
                (queries_hbm, queries_ref),
                (cent_half, cent_ref),
                (codes_hbm, codes_out),
                (length_hbm, length_out),
                (resid_hbm, resid_out),
            )
        )
    ]
    for move in moves:
        move.start()

    def clear(i, carry):
        count_ref[i] = 0
        return carry

    lax.fori_loop(0, peers, clear, 0)
    for move in moves[:4]:
        move.wait()
    row = lax.broadcasted_iota(jnp.int32, req_ref.shape, 0)
    lane = lax.broadcasted_iota(jnp.int32, req_ref.shape, 1)
    req = jnp.full(req_ref.shape, -1, jnp.int32)
    for q in range(q_dev):
        for k in range(per_query):
            owner = owner_ref[q, k]
            slot = count_ref[owner]
            count_ref[owner] = slot + 1
            here = row == owner
            req = jnp.where(here & (lane == slot), local_ref[q, k], req)
            req = jnp.where(here & (lane == slot + dim // 2), q * per_query + k, req)
    req_ref[...] = req.astype(jnp.float32)
    qnorm = normalize(queries_ref[...].reshape(qrows, dim).astype(jnp.float32)).astype(jnp.bfloat16)

    def send(d, carry):
        out_ref[d, :qrows, :] = qnorm
        out_ref[d, qrows : qrows + half, :] = cent_ref[...]
        asked = req_ref[pl.ds(d, PAD), :]
        out_ref[d, qrows + half :, :] = asked.astype(jnp.bfloat16)
        return carry

    lax.fori_loop(0, copies, send, 0)
    for move in moves[4:]:
        move.wait()


def score_kernel(slots, q_dev, per_query, qtok, order, req_ref, length_ref, codes_any, *refs):
    (*parts, other_ref, resid_ref, out_ref) = refs[:-9]
    query_ref, table_ref, rows_ref, best_ref, near_ref, cand_ref, units_ref, codes_ref, sem = refs[-9:]
    peers, half, dim = other_ref.shape
    qrows = q_dev * qtok
    passages, seq = resid_ref.shape[:2]
    pieces = seq // UNIT
    shard = 2 * half
    total = peers * slots
    me = lax.axis_index("index")
    core = lax.axis_index("query")

    bring = pltpu.make_async_copy(codes_any, codes_ref, sem)
    bring.start()
    best_ref[...] = jnp.full(best_ref.shape, -1000000000.0, jnp.float32)
    near_ref[...] = jnp.full(near_ref.shape, -1000000000.0, jnp.float32)

    piece_bits = (pieces - 1).bit_length()
    pass_bits = (passages - 1).bit_length()
    slot_bits = total.bit_length()
    cand_bits = (per_query - 1).bit_length()
    slot_at = piece_bits + pass_bits
    head_at = slot_at + slot_bits

    def field(word, at, bits):
        return lax.shift_right_logical(word, at) & ((1 << bits) - 1)

    def listing(b, n):
        asked = [req_ref[b, s] for s in range(slots)]
        cands = [req_ref[b, s + dim // 2] for s in range(slots)]
        lengths = [jnp.where(p >= 0, length_ref[jnp.maximum(p, 0)], 0) for p in asked]
        for s, (p, c, length) in enumerate(zip(asked, cands, lengths)):
            slot = b * slots + s
            cand_ref[pl.ds(slot, 1), :] = jnp.full((1, dim), c, jnp.int32)
            head = b * q_dev + lax.shift_right_logical(c, cand_bits)
            word = (head << head_at) + (slot << slot_at) + (p << piece_bits)
            for u in range(pieces):
                units_ref[n] = word + u
                n = n + jnp.where(length > u * UNIT, 1, 0)
        return n

    count = lax.fori_loop(0, peers, listing, 0)
    for u in range(GROUP):
        units_ref[count + u] = total << slot_at

    def place(t, part, swapped):
        peer = me ^ order[t] if order else t
        first = pl.multiple_of(peer * shard + core * half, 8)
        second = pl.multiple_of(peer * shard + half - core * half, 8)
        table_ref[pl.ds(first, half), :] = part[qrows : qrows + half, :].astype(jnp.float32)
        table_ref[pl.ds(second, half), :] = swapped[...].astype(jnp.float32)
        query_ref[pl.ds(pl.multiple_of(t * qrows, 16), qrows), :] = part[:qrows, :]

    def place_loop(t, carry):
        place(t, parts[0].at[t], other_ref.at[t])
        return carry

    if order:
        for t in range(peers):
            place(t, parts[t], other_ref.at[t])
    else:
        lax.fori_loop(0, peers, place_loop, 0)

    token = lax.broadcasted_iota(jnp.int32, (UNIT, qtok), 0)
    nt = (((1,), (1,)), ((), ()))

    def fetch(g, carry):
        for j in range(FETCH):
            unit = g * FETCH + j
            word = units_ref[unit]
            base = field(word, 0, piece_bits) * (UNIT * passages) + field(word, piece_bits, pass_bits)
            rows = rows_ref.at[pl.ds(pl.multiple_of(unit * UNIT, UNIT), UNIT)]
            for t in range(UNIT):
                rows[t : t + 1, :] = table_ref[pl.ds(codes_ref[base + t * passages], 1), :]
        return carry

    def compare(g, carry):
        found = []
        for j in range(GROUP):
            unit = g * GROUP + j
            word = units_ref[unit]
            piece = field(word, 0, piece_bits)
            p = field(word, piece_bits, pass_bits)
            row = piece * (total + 8) + field(word, slot_at, slot_bits)
            head = lax.shift_right_logical(word, head_at)
            resid = resid_ref[p, pl.ds(pl.multiple_of(piece * UNIT, UNIT), UNIT), :]
            query = query_ref[pl.ds(pl.multiple_of(head * qtok, qtok), qtok), :]
            left = length_ref[p] - piece * UNIT
            cent = rows_ref[pl.ds(pl.multiple_of(unit * UNIT, UNIT), UNIT), :]
            v = cent + resid.astype(jnp.float32)
            both = jnp.concatenate([normalize(v).astype(jnp.bfloat16), cent.astype(jnp.bfloat16)], axis=0)
            sims = lax.dot_general(both, query, nt, preferred_element_type=jnp.float32)
            tops = [
                jnp.max(jnp.where(token < left, sims[o : o + UNIT], -1000000000.0), axis=0, keepdims=True)
                for o in (0, UNIT)
            ]
            found.append((row, tops))
        for row, (exact, approx) in found:
            best_ref[pl.ds(row, 1), :] = exact
            near_ref[pl.ds(row, 1), :] = approx
        return carry

    bring.wait()
    lax.fori_loop(0, (count + FETCH - 1) // FETCH, fetch, 0)
    lax.fori_loop(0, (count + GROUP - 1) // GROUP, compare, 0)

    def score(ref):
        best = ref[:total, :]
        for u in range(1, pieces):
            best = jnp.maximum(best, ref[u * (total + 8) : u * (total + 8) + total, :])
        return jnp.sum(best, axis=1, keepdims=True)

    cand = cand_ref[...]
    lane = lax.broadcasted_iota(jnp.int32, (total, dim), 1)
    placed = jnp.where(lane == cand, score(best_ref), 0.0)
    placed += jnp.where(lane == cand + q_dev * per_query, score(near_ref), 0.0)
    placed = jnp.where(cand >= 0, placed, 0.0)
    placed = jnp.sum(placed.reshape(peers, slots, dim), axis=1)
    turned = [placed] + [pltpu.roll(placed, dim - r * per_query, 1) for r in range(1, 2 * q_dev)]
    for b in range(peers):
        to = me ^ order[b] if order else b
        for r in range(2 * q_dev):
            out_ref[to, r : r + 1, :] = turned[r][b : b + 1, :]


def body(queries, cand_owner, cand_local, centroids, passage_codes, residuals, passage_lengths):
    peers = lax.axis_size("index")
    cores = lax.axis_size("query")
    q_dev, per_query = cand_owner.shape
    count = q_dev * per_query
    slots = max(2, (2 * count + peers - 1) // peers)
    seq, dim = residuals.shape[1:]
    qtok = queries.shape[1]
    qrows = q_dev * qtok
    half = centroids.shape[0] // cores
    rows = qrows + half + PAD
    order = tuple(range(peers - 1, -1, -1)) if peers <= PAD and peers & (peers - 1) == 0 else ()
    vmem = pl.BlockSpec(memory_space=pltpu.VMEM)
    smem = pl.BlockSpec(memory_space=pltpu.SMEM)
    hbm = pl.BlockSpec(memory_space=pltpu.HBM)
    copies = 1 if order else peers
    pack_mib = 2 * copies * rows * dim * 2 // MIB
    held = [passage_codes.T.reshape(-1), residuals, passage_lengths]
    inputs = [cand_owner, cand_local, queries, centroids] + held
    packed, *held = pl.pallas_call(
        pack_kernel,
        out_shape=[jax.ShapeDtypeStruct((copies, rows, dim), jnp.bfloat16)]
        + [jax.ShapeDtypeStruct(x.shape, x.dtype) for x in held],
        in_specs=[hbm] * 7,
        out_specs=[vmem] * 4,
        scratch_shapes=[
            pltpu.SMEM((peers,), jnp.int32),
            pltpu.VMEM((peers + PAD, dim), jnp.float32),
            pltpu.SMEM(cand_owner.shape, jnp.int32),
            pltpu.SMEM(cand_local.shape, jnp.int32),
            pltpu.VMEM(queries.shape, queries.dtype),
            pltpu.VMEM((half, dim), centroids.dtype),
            pltpu.SemaphoreType.DMA((7,)),
        ],
        compiler_params=pltpu.CompilerParams(vmem_limit_bytes=(8 + pack_mib) * MIB),
    )(*(pltpu.with_memory_space_constraint(x, pltpu.HBM) for x in inputs))
    codes, resid, lengths = held
    if order:
        parts = [
            lax.ppermute(packed[0], "index", [(i, i ^ t) for i in range(peers)]) if t else packed[0]
            for t in order
        ]
        mine = jnp.stack([part[qrows : qrows + half] for part in parts])
        asked = jnp.stack([part[qrows + half :] for part in parts])
        asked = lax.dynamic_index_in_dim(asked, lax.axis_index("index"), 1, keepdims=False)
    else:
        parts = [lax.all_to_all(packed, "index", split_axis=0, concat_axis=0, tiled=True)]
        mine = parts[0][:, qrows : qrows + half]
        asked = parts[0][:, qrows + half]
    other = lax.ppermute(mine, "query", [(0, 1), (1, 0)])
    table_mib = 2 * peers * half * dim * 2 // MIB
    bests = (seq // UNIT) * (peers * slots + 8)
    scores = pl.pallas_call(
        functools.partial(score_kernel, slots, q_dev, per_query, qtok, order),
        out_shape=jax.ShapeDtypeStruct((peers, 2 * q_dev, dim), jnp.float32),
        in_specs=[smem, smem, pl.BlockSpec(memory_space=pl.ANY)] + [vmem] * (len(parts) + 2),
        out_specs=vmem,
        scratch_shapes=[
            pltpu.VMEM((peers * qrows, dim), jnp.bfloat16),
            pltpu.VMEM((peers * cores * half, dim), jnp.float32),
            pltpu.VMEM((peers * slots * seq + GROUP * UNIT, dim), jnp.float32),
            pltpu.VMEM((bests, qtok), jnp.float32),
            pltpu.VMEM((bests, qtok), jnp.float32),
            pltpu.VMEM((peers * slots, dim), jnp.int32),
            pltpu.SMEM((peers * slots * (seq // UNIT) + GROUP,), jnp.int32),
            pltpu.SMEM(codes.shape, jnp.int32),
            pltpu.SemaphoreType.DMA,
        ],
        compiler_params=pltpu.CompilerParams(vmem_limit_bytes=(12 + 4 * table_mib + peers * slots * seq * dim * 4 // MIB) * MIB),
    )(asked.astype(jnp.int32), lengths, codes, *parts, other, resid)
    back = lax.all_to_all(scores, "index", split_axis=0, concat_axis=0, tiled=True)
    result = jnp.sum(back[:, :, :per_query], axis=0)
    return result[:q_dev], result[q_dev:]


def solution(mesh):
    in_specs = (
        P(("group", "index", "query"), None, None),
        P(("group", "index", "query"), None),
        P(("group", "index", "query"), None),
        P("index", None),
        P("index", None),
        P("index", None, None),
        P("index"),
    )
    out_specs = (P(("group", "index", "query"), None), P(("group", "index", "query"), None))
    return jax.shard_map(body, mesh=mesh, in_specs=in_specs, out_specs=out_specs, check_vma=False)
```

```python
import functools

import jax
import jax.numpy as jnp
from jax import lax
from jax.experimental import pallas as pl
from jax.experimental.pallas import tpu as pltpu
from jax.sharding import PartitionSpec as P

EPS = 1e-06
PAD = 16
UNIT = 32
GROUP = 32
FETCH = 8
MIB = 1024 * 1024


def normalize(wide):
    return wide * lax.rsqrt(jnp.sum(wide * wide, axis=-1, keepdims=True) + EPS)


def pack_kernel(
    owner_hbm,
    local_hbm,
    queries_hbm,
    cent_hbm,
    codes_hbm,
    length_hbm,
    out_ref,
    codes_out,
    length_out,
    count_ref,
    req_ref,
    owner_ref,
    local_ref,
    queries_ref,
    cent_ref,
    sems,
):
    copies = out_ref.shape[0]
    peers = count_ref.shape[0]
    q_dev, per_query = owner_ref.shape
    qrows = queries_ref.shape[0] * queries_ref.shape[1]
    half, dim = cent_ref.shape
    core = lax.axis_index("query")
    cent_half = cent_hbm.at[pl.ds(pl.multiple_of(core * half, 16), half)]
    moves = [
        pltpu.make_async_copy(src, dst, sems.at[i])
        for i, (src, dst) in enumerate(
            (
                (owner_hbm, owner_ref),
                (local_hbm, local_ref),
                (queries_hbm, queries_ref),
                (cent_half, cent_ref),
                (codes_hbm, codes_out),
                (length_hbm, length_out),
            )
        )
    ]
    for move in moves:
        move.start()

    def clear(i, carry):
        count_ref[i] = 0
        return carry

    lax.fori_loop(0, peers, clear, 0)
    for move in moves[:4]:
        move.wait()
    row = lax.broadcasted_iota(jnp.int32, req_ref.shape, 0)
    lane = lax.broadcasted_iota(jnp.int32, req_ref.shape, 1)
    req = jnp.full(req_ref.shape, -1, jnp.int32)
    for q in range(q_dev):
        for k in range(per_query):
            owner = owner_ref[q, k]
            slot = count_ref[owner]
            count_ref[owner] = slot + 1
            here = row == owner
            req = jnp.where(here & (lane == slot), local_ref[q, k], req)
            req = jnp.where(here & (lane == slot + dim // 2), q * per_query + k, req)
    req_ref[...] = req.astype(jnp.float32)
    qnorm = normalize(queries_ref[...].reshape(qrows, dim).astype(jnp.float32)).astype(jnp.bfloat16)

    def send(d, carry):
        out_ref[d, :qrows, :] = qnorm
        out_ref[d, qrows : qrows + half, :] = cent_ref[...]
        asked = req_ref[pl.ds(d, PAD), :]
        out_ref[d, qrows + half :, :] = asked.astype(jnp.bfloat16)
        return carry

    lax.fori_loop(0, copies, send, 0)
    for move in moves[4:]:
        move.wait()


def score_kernel(slots, q_dev, per_query, qtok, order, req_ref, length_ref, codes_any, *refs):
    (*parts, other_ref, resid_hbm, out_ref) = refs[:-10]
    query_ref, table_ref, rows_ref, best_ref, near_ref, cand_ref, units_ref, codes_ref, resid_ref, sems = refs[-10:]
    peers, half, dim = other_ref.shape
    qrows = q_dev * qtok
    passages, seq = resid_hbm.shape[:2]
    pieces = seq // UNIT
    shard = 2 * half
    total = peers * slots
    me = lax.axis_index("index")
    core = lax.axis_index("query")

    bring_codes = pltpu.make_async_copy(codes_any, codes_ref, sems.at[0])
    bring_codes.start()
    bring_resid = pltpu.make_async_copy(resid_hbm, resid_ref, sems.at[1])
    bring_resid.start()
    best_ref[...] = jnp.full(best_ref.shape, -1000000000.0, jnp.float32)
    near_ref[...] = jnp.full(near_ref.shape, -1000000000.0, jnp.float32)

    piece_bits = (pieces - 1).bit_length()
    pass_bits = (passages - 1).bit_length()
    slot_bits = total.bit_length()
    cand_bits = (per_query - 1).bit_length()
    slot_at = piece_bits + pass_bits
    head_at = slot_at + slot_bits

    def field(word, at, bits):
        return lax.shift_right_logical(word, at) & ((1 << bits) - 1)

    def listing(b, n):
        asked = [req_ref[b, s] for s in range(slots)]
        cands = [req_ref[b, s + dim // 2] for s in range(slots)]
        lengths = [jnp.where(p >= 0, length_ref[jnp.maximum(p, 0)], 0) for p in asked]
        for s, (p, c, length) in enumerate(zip(asked, cands, lengths)):
            slot = b * slots + s
            cand_ref[pl.ds(slot, 1), :] = jnp.full((1, dim), c, jnp.int32)
            head = b * q_dev + lax.shift_right_logical(c, cand_bits)
            word = (head << head_at) + (slot << slot_at) + (p << piece_bits)
            for u in range(pieces):
                units_ref[n] = word + u
                n = n + jnp.where(length > u * UNIT, 1, 0)
        return n

    count = lax.fori_loop(0, peers, listing, 0)
    for u in range(GROUP):
        units_ref[count + u] = total << slot_at

    def place(t, part, swapped):
        peer = me ^ order[t] if order else t
        first = pl.multiple_of(peer * shard + core * half, 8)
        second = pl.multiple_of(peer * shard + half - core * half, 8)
        table_ref[pl.ds(first, half), :] = part[qrows : qrows + half, :].astype(jnp.float32)
        table_ref[pl.ds(second, half), :] = swapped[...].astype(jnp.float32)
        query_ref[pl.ds(pl.multiple_of(t * qrows, 16), qrows), :] = part[:qrows, :]

    def place_loop(t, carry):
        place(t, parts[0].at[t], other_ref.at[t])
        return carry

    if order:
        for t in range(peers):
            place(t, parts[t], other_ref.at[t])
    else:
        lax.fori_loop(0, peers, place_loop, 0)

    token = lax.broadcasted_iota(jnp.int32, (UNIT, qtok), 0)
    nt = (((1,), (1,)), ((), ()))

    def fetch(g, carry):
        for j in range(FETCH):
            unit = g * FETCH + j
            word = units_ref[unit]
            base = field(word, 0, piece_bits) * (UNIT * passages) + field(word, piece_bits, pass_bits)
            rows = rows_ref.at[pl.ds(pl.multiple_of(unit * UNIT, UNIT), UNIT)]
            for t in range(UNIT):
                rows[t : t + 1, :] = table_ref[pl.ds(codes_ref[base + t * passages], 1), :]
        return carry

    def compare(g, carry):
        found = []
        for j in range(GROUP):
            unit = g * GROUP + j
            word = units_ref[unit]
            piece = field(word, 0, piece_bits)
            p = field(word, piece_bits, pass_bits)
            row = piece * (total + 8) + field(word, slot_at, slot_bits)
            head = lax.shift_right_logical(word, head_at)
            resid = resid_ref[p, pl.ds(pl.multiple_of(piece * UNIT, UNIT), UNIT), :]
            query = query_ref[pl.ds(pl.multiple_of(head * qtok, qtok), qtok), :]
            left = length_ref[p] - piece * UNIT
            cent = rows_ref[pl.ds(pl.multiple_of(unit * UNIT, UNIT), UNIT), :]
            v = cent + resid.astype(jnp.float32)
            both = jnp.concatenate([normalize(v).astype(jnp.bfloat16), cent.astype(jnp.bfloat16)], axis=0)
            sims = lax.dot_general(both, query, nt, preferred_element_type=jnp.float32)
            tops = [
                jnp.max(jnp.where(token < left, sims[o : o + UNIT], -1000000000.0), axis=0, keepdims=True)
                for o in (0, UNIT)
            ]
            found.append((row, tops))
        for row, (exact, approx) in found:
            best_ref[pl.ds(row, 1), :] = exact
            near_ref[pl.ds(row, 1), :] = approx
        return carry

    bring_codes.wait()
    lax.fori_loop(0, (count + FETCH - 1) // FETCH, fetch, 0)
    bring_resid.wait()
    lax.fori_loop(0, (count + GROUP - 1) // GROUP, compare, 0)

    def score(ref):
        best = ref[:total, :]
        for u in range(1, pieces):
            best = jnp.maximum(best, ref[u * (total + 8) : u * (total + 8) + total, :])
        return jnp.sum(best, axis=1, keepdims=True)

    cand = cand_ref[...]
    lane = lax.broadcasted_iota(jnp.int32, (total, dim), 1)
    placed = jnp.where(lane == cand, score(best_ref), 0.0)
    placed += jnp.where(lane == cand + q_dev * per_query, score(near_ref), 0.0)
    placed = jnp.where(cand >= 0, placed, 0.0)
    placed = jnp.sum(placed.reshape(peers, slots, dim), axis=1)
    turned = [placed] + [pltpu.roll(placed, dim - r * per_query, 1) for r in range(1, 2 * q_dev)]
    for b in range(peers):
        to = me ^ order[b] if order else b
        for r in range(2 * q_dev):
            out_ref[to, r : r + 1, :] = turned[r][b : b + 1, :]


def body(queries, cand_owner, cand_local, centroids, passage_codes, residuals, passage_lengths):
    peers = lax.axis_size("index")
    cores = lax.axis_size("query")
    q_dev, per_query = cand_owner.shape
    count = q_dev * per_query
    slots = max(2, (2 * count + peers - 1) // peers)
    seq, dim = residuals.shape[1:]
    qtok = queries.shape[1]
    qrows = q_dev * qtok
    half = centroids.shape[0] // cores
    rows = qrows + half + PAD
    order = tuple(range(peers - 1, -1, -1)) if peers <= PAD and peers & (peers - 1) == 0 else ()
    vmem = pl.BlockSpec(memory_space=pltpu.VMEM)
    smem = pl.BlockSpec(memory_space=pltpu.SMEM)
    hbm = pl.BlockSpec(memory_space=pltpu.HBM)
    copies = 1 if order else peers
    pack_mib = 2 * copies * rows * dim * 2 // MIB
    held = [passage_codes.T.reshape(-1), passage_lengths]
    inputs = [cand_owner, cand_local, queries, centroids] + held
    packed, *held = pl.pallas_call(
        pack_kernel,
        out_shape=[jax.ShapeDtypeStruct((copies, rows, dim), jnp.bfloat16)]
        + [jax.ShapeDtypeStruct(x.shape, x.dtype) for x in held],
        in_specs=[hbm] * 6,
        out_specs=[vmem] * 3,
        scratch_shapes=[
            pltpu.SMEM((peers,), jnp.int32),
            pltpu.VMEM((peers + PAD, dim), jnp.float32),
            pltpu.SMEM(cand_owner.shape, jnp.int32),
            pltpu.SMEM(cand_local.shape, jnp.int32),
            pltpu.VMEM(queries.shape, queries.dtype),
            pltpu.VMEM((half, dim), centroids.dtype),
            pltpu.SemaphoreType.DMA((6,)),
        ],
        compiler_params=pltpu.CompilerParams(vmem_limit_bytes=(8 + pack_mib) * MIB),
    )(*(pltpu.with_memory_space_constraint(x, pltpu.HBM) for x in inputs))
    codes, lengths = held
    resid = pltpu.with_memory_space_constraint(residuals, pltpu.HBM)
    if order:
        parts = [
            lax.ppermute(packed[0], "index", [(i, i ^ t) for i in range(peers)]) if t else packed[0]
            for t in order
        ]
        mine = jnp.stack([part[qrows : qrows + half] for part in parts])
        asked = jnp.stack([part[qrows + half :] for part in parts])
        asked = lax.dynamic_index_in_dim(asked, lax.axis_index("index"), 1, keepdims=False)
    else:
        parts = [lax.all_to_all(packed, "index", split_axis=0, concat_axis=0, tiled=True)]
        mine = parts[0][:, qrows : qrows + half]
        asked = parts[0][:, qrows + half]
    other = lax.ppermute(mine, "query", [(0, 1), (1, 0)])
    table_mib = 2 * peers * half * dim * 2 // MIB
    bests = (seq // UNIT) * (peers * slots + 8)
    scores = pl.pallas_call(
        functools.partial(score_kernel, slots, q_dev, per_query, qtok, order),
        out_shape=jax.ShapeDtypeStruct((peers, 2 * q_dev, dim), jnp.float32),
        in_specs=[smem, smem, pl.BlockSpec(memory_space=pl.ANY)] + [vmem] * (len(parts) + 1) + [hbm],
        out_specs=vmem,
        scratch_shapes=[
            pltpu.VMEM((peers * qrows, dim), jnp.bfloat16),
            pltpu.VMEM((peers * cores * half, dim), jnp.float32),
            pltpu.VMEM((peers * slots * seq + GROUP * UNIT, dim), jnp.float32),
            pltpu.VMEM((bests, qtok), jnp.float32),
            pltpu.VMEM((bests, qtok), jnp.float32),
            pltpu.VMEM((peers * slots, dim), jnp.int32),
            pltpu.SMEM((peers * slots * (seq // UNIT) + GROUP,), jnp.int32),
            pltpu.SMEM(codes.shape, jnp.int32),
            pltpu.VMEM(residuals.shape, residuals.dtype),
            pltpu.SemaphoreType.DMA((2,)),
        ],
        compiler_params=pltpu.CompilerParams(vmem_limit_bytes=(12 + 4 * table_mib + peers * slots * seq * dim * 4 // MIB) * MIB),
    )(asked.astype(jnp.int32), lengths, codes, *parts, other, resid)
    back = lax.all_to_all(scores, "index", split_axis=0, concat_axis=0, tiled=True)
    result = jnp.sum(back[:, :, :per_query], axis=0)
    return result[:q_dev], result[q_dev:]


def solution(mesh):
    in_specs = (
        P(("group", "index", "query"), None, None),
        P(("group", "index", "query"), None),
        P(("group", "index", "query"), None),
        P("index", None),
        P("index", None),
        P("index", None, None),
        P("index"),
    )
    out_specs = (P(("group", "index", "query"), None), P(("group", "index", "query"), None))
    return jax.shard_map(body, mesh=mesh, in_specs=in_specs, out_specs=out_specs, check_vma=False)
```

```python
import functools

import jax
import jax.numpy as jnp
from jax import lax
from jax.experimental import pallas as pl
from jax.experimental.pallas import tpu as pltpu
from jax.sharding import PartitionSpec as P

EPS = 1e-06
PAD = 16
UNIT = 32
GROUP = 32
ORDER = (4, 6, 1, 3, 2, 5, 7, 0)
RELAYED = (5, 7)
FETCH = 8
MIB = 1024 * 1024


def normalize(wide):
    return wide * lax.rsqrt(jnp.sum(wide * wide, axis=-1, keepdims=True) + EPS)


def pack_kernel(
    owner_hbm,
    local_hbm,
    queries_hbm,
    cent_hbm,
    codes_hbm,
    length_hbm,
    out_ref,
    codes_out,
    length_out,
    count_ref,
    req_ref,
    owner_ref,
    local_ref,
    queries_ref,
    cent_ref,
    sems,
):
    copies = out_ref.shape[0]
    peers = count_ref.shape[0]
    q_dev, per_query = owner_ref.shape
    qrows = queries_ref.shape[0] * queries_ref.shape[1]
    half, dim = cent_ref.shape
    core = lax.axis_index("query")
    cent_half = cent_hbm.at[pl.ds(pl.multiple_of(core * half, 16), half)]
    moves = [
        pltpu.make_async_copy(src, dst, sems.at[i])
        for i, (src, dst) in enumerate(
            (
                (owner_hbm, owner_ref),
                (local_hbm, local_ref),
                (queries_hbm, queries_ref),
                (cent_half, cent_ref),
                (codes_hbm, codes_out),
                (length_hbm, length_out),
            )
        )
    ]
    for move in moves:
        move.start()

    def clear(i, carry):
        count_ref[i] = 0
        return carry

    lax.fori_loop(0, peers, clear, 0)
    for move in moves[:4]:
        move.wait()
    row = lax.broadcasted_iota(jnp.int32, req_ref.shape, 0)
    lane = lax.broadcasted_iota(jnp.int32, req_ref.shape, 1)
    req = jnp.full(req_ref.shape, -1, jnp.int32)
    for q in range(q_dev):
        for k in range(per_query):
            owner = owner_ref[q, k]
            slot = count_ref[owner]
            count_ref[owner] = slot + 1
            here = row == owner
            req = jnp.where(here & (lane == slot), local_ref[q, k], req)
            req = jnp.where(here & (lane == slot + dim // 2), q * per_query + k, req)
    req_ref[...] = req.astype(jnp.float32)
    qnorm = normalize(queries_ref[...].reshape(qrows, dim).astype(jnp.float32)).astype(jnp.bfloat16)

    def send(d, carry):
        out_ref[d, :qrows, :] = qnorm
        out_ref[d, qrows : qrows + half, :] = cent_ref[...]
        asked = req_ref[pl.ds(d, PAD), :]
        out_ref[d, qrows + half :, :] = asked.astype(jnp.bfloat16)
        return carry

    lax.fori_loop(0, copies, send, 0)
    for move in moves[4:]:
        move.wait()


def score_kernel(slots, q_dev, per_query, qtok, order, req_ref, length_ref, codes_any, *refs):
    (*parts, other_ref, resid_hbm, out_ref) = refs[:-10]
    query_ref, table_ref, rows_ref, best_ref, near_ref, cand_ref, units_ref, codes_ref, resid_ref, sems = refs[-10:]
    peers, half, dim = other_ref.shape
    qrows = q_dev * qtok
    passages, seq = resid_hbm.shape[:2]
    pieces = seq // UNIT
    shard = 2 * half
    total = peers * slots
    me = lax.axis_index("index")
    core = lax.axis_index("query")

    bring_codes = pltpu.make_async_copy(codes_any, codes_ref, sems.at[0])
    bring_codes.start()
    bring_resid = pltpu.make_async_copy(resid_hbm, resid_ref, sems.at[1])
    bring_resid.start()
    best_ref[...] = jnp.full(best_ref.shape, -1000000000.0, jnp.float32)
    near_ref[...] = jnp.full(near_ref.shape, -1000000000.0, jnp.float32)

    piece_bits = (pieces - 1).bit_length()
    pass_bits = (passages - 1).bit_length()
    slot_bits = total.bit_length()
    cand_bits = (per_query - 1).bit_length()
    slot_at = piece_bits + pass_bits
    head_at = slot_at + slot_bits

    def field(word, at, bits):
        return lax.shift_right_logical(word, at) & ((1 << bits) - 1)

    def listing(b, n):
        asked = [req_ref[b, s] for s in range(slots)]
        cands = [req_ref[b, s + dim // 2] for s in range(slots)]
        lengths = [jnp.where(p >= 0, length_ref[jnp.maximum(p, 0)], 0) for p in asked]
        for s, (p, c, length) in enumerate(zip(asked, cands, lengths)):
            slot = b * slots + s
            cand_ref[pl.ds(slot, 1), :] = jnp.full((1, dim), c, jnp.int32)
            head = b * q_dev + lax.shift_right_logical(c, cand_bits)
            word = (head << head_at) + (slot << slot_at) + (p << piece_bits)
            for u in range(pieces):
                units_ref[n] = word + u
                n = n + jnp.where(length > u * UNIT, 1, 0)
        return n

    count = lax.fori_loop(0, peers, listing, 0)
    for u in range(GROUP):
        units_ref[count + u] = total << slot_at

    def place(t, part, swapped):
        peer = me ^ order[t] if order else t
        first = pl.multiple_of(peer * shard + core * half, 8)
        second = pl.multiple_of(peer * shard + half - core * half, 8)
        table_ref[pl.ds(first, half), :] = part[qrows : qrows + half, :].astype(jnp.float32)
        table_ref[pl.ds(second, half), :] = swapped[...].astype(jnp.float32)
        query_ref[pl.ds(pl.multiple_of(t * qrows, 16), qrows), :] = part[:qrows, :]

    def place_loop(t, carry):
        place(t, parts[0].at[t], other_ref.at[t])
        return carry

    if order:
        for t in range(peers):
            place(t, parts[t], other_ref.at[t])
    else:
        lax.fori_loop(0, peers, place_loop, 0)

    token = lax.broadcasted_iota(jnp.int32, (UNIT, qtok), 0)
    nt = (((1,), (1,)), ((), ()))

    def fetch(g, carry):
        for j in range(FETCH):
            unit = g * FETCH + j
            word = units_ref[unit]
            base = field(word, 0, piece_bits) * (UNIT * passages) + field(word, piece_bits, pass_bits)
            rows = rows_ref.at[pl.ds(pl.multiple_of(unit * UNIT, UNIT), UNIT)]
            for t in range(UNIT):
                rows[t : t + 1, :] = table_ref[pl.ds(codes_ref[base + t * passages], 1), :]
        return carry

    def compare(g, carry):
        found = []
        for j in range(GROUP):
            unit = g * GROUP + j
            word = units_ref[unit]
            piece = field(word, 0, piece_bits)
            p = field(word, piece_bits, pass_bits)
            row = piece * (total + 8) + field(word, slot_at, slot_bits)
            head = lax.shift_right_logical(word, head_at)
            resid = resid_ref[p, pl.ds(pl.multiple_of(piece * UNIT, UNIT), UNIT), :]
            query = query_ref[pl.ds(pl.multiple_of(head * qtok, qtok), qtok), :]
            left = length_ref[p] - piece * UNIT
            cent = rows_ref[pl.ds(pl.multiple_of(unit * UNIT, UNIT), UNIT), :]
            v = cent + resid.astype(jnp.float32)
            both = jnp.concatenate([normalize(v).astype(jnp.bfloat16), cent.astype(jnp.bfloat16)], axis=0)
            sims = lax.dot_general(both, query, nt, preferred_element_type=jnp.float32)
            tops = [
                jnp.max(jnp.where(token < left, sims[o : o + UNIT], -1000000000.0), axis=0, keepdims=True)
                for o in (0, UNIT)
            ]
            found.append((row, tops))
        for row, (exact, approx) in found:
            best_ref[pl.ds(row, 1), :] = exact
            near_ref[pl.ds(row, 1), :] = approx
        return carry

    bring_codes.wait()
    lax.fori_loop(0, (count + FETCH - 1) // FETCH, fetch, 0)
    bring_resid.wait()
    lax.fori_loop(0, (count + GROUP - 1) // GROUP, compare, 0)

    def score(ref):
        best = ref[:total, :]
        for u in range(1, pieces):
            best = jnp.maximum(best, ref[u * (total + 8) : u * (total + 8) + total, :])
        return jnp.sum(best, axis=1, keepdims=True)

    cand = cand_ref[...]
    lane = lax.broadcasted_iota(jnp.int32, (total, dim), 1)
    placed = jnp.where(lane == cand, score(best_ref), 0.0)
    placed += jnp.where(lane == cand + q_dev * per_query, score(near_ref), 0.0)
    placed = jnp.where(cand >= 0, placed, 0.0)
    placed = jnp.sum(placed.reshape(peers, slots, dim), axis=1)
    turned = [placed] + [pltpu.roll(placed, dim - r * per_query, 1) for r in range(1, 2 * q_dev)]
    for b in range(peers):
        to = me ^ order[b] if order else b
        for r in range(2 * q_dev):
            out_ref[to, r : r + 1, :] = turned[r][b : b + 1, :]


def body(queries, cand_owner, cand_local, centroids, passage_codes, residuals, passage_lengths):
    peers = lax.axis_size("index")
    cores = lax.axis_size("query")
    q_dev, per_query = cand_owner.shape
    count = q_dev * per_query
    slots = max(2, (2 * count + peers - 1) // peers)
    seq, dim = residuals.shape[1:]
    qtok = queries.shape[1]
    qrows = q_dev * qtok
    half = centroids.shape[0] // cores
    rows = qrows + half + PAD
    order = ORDER if peers == len(ORDER) else ()
    vmem = pl.BlockSpec(memory_space=pltpu.VMEM)
    smem = pl.BlockSpec(memory_space=pltpu.SMEM)
    hbm = pl.BlockSpec(memory_space=pltpu.HBM)
    copies = 1 if order else peers
    pack_mib = 2 * copies * rows * dim * 2 // MIB
    held = [passage_codes.T.reshape(-1), passage_lengths]
    inputs = [cand_owner, cand_local, queries, centroids] + held
    packed, *held = pl.pallas_call(
        pack_kernel,
        out_shape=[jax.ShapeDtypeStruct((copies, rows, dim), jnp.bfloat16)]
        + [jax.ShapeDtypeStruct(x.shape, x.dtype) for x in held],
        in_specs=[hbm] * 6,
        out_specs=[vmem] * 3,
        scratch_shapes=[
            pltpu.SMEM((peers,), jnp.int32),
            pltpu.VMEM((peers + PAD, dim), jnp.float32),
            pltpu.SMEM(cand_owner.shape, jnp.int32),
            pltpu.SMEM(cand_local.shape, jnp.int32),
            pltpu.VMEM(queries.shape, queries.dtype),
            pltpu.VMEM((half, dim), centroids.dtype),
            pltpu.SemaphoreType.DMA((6,)),
        ],
        compiler_params=pltpu.CompilerParams(vmem_limit_bytes=(8 + pack_mib) * MIB),
    )(*(pltpu.with_memory_space_constraint(x, pltpu.HBM) for x in inputs))
    codes, lengths = held
    resid = pltpu.with_memory_space_constraint(residuals, pltpu.HBM)
    if order:
        swap = lambda x, t: lax.ppermute(x, "index", [(i, i ^ t) for i in range(peers)])
        known = {0: packed[0]}
        for t in order:
            if t not in known and t not in RELAYED:
                known[t] = swap(known[0], t)
        for t in RELAYED:
            known[t] = swap(known[t ^ 1], 1)
        parts = [known[t] for t in order]
        mine = jnp.stack([part[qrows : qrows + half] for part in parts])
        asked = jnp.stack([part[qrows + half :] for part in parts])
        asked = lax.dynamic_index_in_dim(asked, lax.axis_index("index"), 1, keepdims=False)
    else:
        parts = [lax.all_to_all(packed, "index", split_axis=0, concat_axis=0, tiled=True)]
        mine = parts[0][:, qrows : qrows + half]
        asked = parts[0][:, qrows + half]
    other = lax.ppermute(mine, "query", [(0, 1), (1, 0)])
    table_mib = 2 * peers * half * dim * 2 // MIB
    bests = (seq // UNIT) * (peers * slots + 8)
    scores = pl.pallas_call(
        functools.partial(score_kernel, slots, q_dev, per_query, qtok, order),
        out_shape=jax.ShapeDtypeStruct((peers, 2 * q_dev, dim), jnp.float32),
        in_specs=[smem, smem, pl.BlockSpec(memory_space=pl.ANY)] + [vmem] * (len(parts) + 1) + [hbm],
        out_specs=vmem,
        scratch_shapes=[
            pltpu.VMEM((peers * qrows, dim), jnp.bfloat16),
            pltpu.VMEM((peers * cores * half, dim), jnp.float32),
            pltpu.VMEM((peers * slots * seq + GROUP * UNIT, dim), jnp.float32),
            pltpu.VMEM((bests, qtok), jnp.float32),
            pltpu.VMEM((bests, qtok), jnp.float32),
            pltpu.VMEM((peers * slots, dim), jnp.int32),
            pltpu.SMEM((peers * slots * (seq // UNIT) + GROUP,), jnp.int32),
            pltpu.SMEM(codes.shape, jnp.int32),
            pltpu.VMEM(residuals.shape, residuals.dtype),
            pltpu.SemaphoreType.DMA((2,)),
        ],
        compiler_params=pltpu.CompilerParams(vmem_limit_bytes=(12 + 4 * table_mib + peers * slots * seq * dim * 4 // MIB) * MIB),
    )(asked.astype(jnp.int32), lengths, codes, *parts, other, resid)
    back = lax.all_to_all(scores, "index", split_axis=0, concat_axis=0, tiled=True)
    result = jnp.sum(back[:, :, :per_query], axis=0)
    return result[:q_dev], result[q_dev:]


def solution(mesh):
    in_specs = (
        P(("group", "index", "query"), None, None),
        P(("group", "index", "query"), None),
        P(("group", "index", "query"), None),
        P("index", None),
        P("index", None),
        P("index", None, None),
        P("index"),
    )
    out_specs = (P(("group", "index", "query"), None), P(("group", "index", "query"), None))
    return jax.shard_map(body, mesh=mesh, in_specs=in_specs, out_specs=out_specs, check_vma=False)
```

```python
import functools

import jax
import jax.numpy as jnp
from jax import lax
from jax.experimental import pallas as pl
from jax.experimental.pallas import tpu as pltpu
from jax.sharding import PartitionSpec as P

EPS = 1e-06
PAD = 16
UNIT = 32
GROUP = 32
ORDER = (4, 6, 1, 3, 2, 5, 7, 0)
RELAYED = (5, 7)
FETCH = 8
MIB = 1024 * 1024


def normalize(wide):
    return wide * lax.rsqrt(jnp.sum(wide * wide, axis=-1, keepdims=True) + EPS)


def pack_kernel(
    owner_hbm,
    local_hbm,
    queries_hbm,
    cent_hbm,
    codes_hbm,
    length_hbm,
    out_ref,
    codes_out,
    length_out,
    codes_ref,
    count_ref,
    req_ref,
    owner_ref,
    local_ref,
    queries_ref,
    cent_ref,
    sems,
):
    copies = out_ref.shape[0]
    peers = count_ref.shape[0]
    q_dev, per_query = owner_ref.shape
    qrows = queries_ref.shape[0] * queries_ref.shape[1]
    half, dim = cent_ref.shape
    core = lax.axis_index("query")
    cent_half = cent_hbm.at[pl.ds(pl.multiple_of(core * half, 16), half)]
    moves = [
        pltpu.make_async_copy(src, dst, sems.at[i])
        for i, (src, dst) in enumerate(
            (
                (owner_hbm, owner_ref),
                (local_hbm, local_ref),
                (queries_hbm, queries_ref),
                (cent_half, cent_ref),
                (codes_hbm, codes_ref),
                (length_hbm, length_out),
            )
        )
    ]
    for move in moves:
        move.start()

    def clear(i, carry):
        count_ref[i] = 0
        return carry

    lax.fori_loop(0, peers, clear, 0)
    for move in moves[:4]:
        move.wait()
    row = lax.broadcasted_iota(jnp.int32, req_ref.shape, 0)
    lane = lax.broadcasted_iota(jnp.int32, req_ref.shape, 1)
    req = jnp.full(req_ref.shape, -1, jnp.int32)
    for q in range(q_dev):
        for k in range(per_query):
            owner = owner_ref[q, k]
            slot = count_ref[owner]
            count_ref[owner] = slot + 1
            here = row == owner
            req = jnp.where(here & (lane == slot), local_ref[q, k], req)
            req = jnp.where(here & (lane == slot + dim // 2), q * per_query + k, req)
    req_ref[...] = req.astype(jnp.float32)
    qnorm = normalize(queries_ref[...].reshape(qrows, dim).astype(jnp.float32)).astype(jnp.bfloat16)

    def send(d, carry):
        out_ref[d, :qrows, :] = qnorm
        out_ref[d, qrows : qrows + half, :] = cent_ref[...]
        asked = req_ref[pl.ds(d, PAD), :]
        out_ref[d, qrows + half :, :] = asked.astype(jnp.bfloat16)
        return carry

    lax.fori_loop(0, copies, send, 0)
    for move in moves[4:]:
        move.wait()
    pair = UNIT // 2
    for u in range(codes_ref.shape[0] // UNIT):
        low = codes_ref[u * UNIT : u * UNIT + pair, :]
        high = codes_ref[u * UNIT + pair : (u + 1) * UNIT, :]
        codes_out[u * pair : (u + 1) * pair, :] = low | (high << 16)


def field_bits(peers, slots, passages, seq):
    return (seq // UNIT - 1).bit_length(), (passages - 1).bit_length(), (peers * slots).bit_length()


def score_kernel(slots, q_dev, per_query, qtok, order, req_ref, length_ref, codes_any, *refs):
    (*parts, other_ref, resid_hbm, out_ref) = refs[:-10]
    query_ref, table_ref, rows_ref, best_ref, near_ref, cand_ref, units_ref, codes_ref, resid_ref, sems = refs[-10:]
    peers, half, dim = other_ref.shape
    qrows = q_dev * qtok
    passages, seq = resid_hbm.shape[:2]
    pieces = seq // UNIT
    shard = 2 * half
    total = peers * slots
    me = lax.axis_index("index")
    core = lax.axis_index("query")

    bring_codes = pltpu.make_async_copy(codes_any, codes_ref, sems.at[0])
    bring_codes.start()
    bring_resid = pltpu.make_async_copy(resid_hbm, resid_ref, sems.at[1])
    bring_resid.start()
    best_ref[...] = jnp.full(best_ref.shape, -1000000000.0, jnp.float32)
    near_ref[...] = jnp.full(near_ref.shape, -1000000000.0, jnp.float32)

    piece_bits, pass_bits, slot_bits = field_bits(peers, slots, passages, seq)
    cand_bits = (per_query - 1).bit_length()
    slot_at = piece_bits + pass_bits
    head_at = slot_at + slot_bits

    def field(word, at, bits):
        return lax.shift_right_logical(word, at) & ((1 << bits) - 1)

    def listing(b, n):
        words = [req_ref[b, s] for s in range(slots)]
        lengths = [jnp.where(w >= 0, length_ref[field(w, piece_bits, pass_bits)], 0) for w in words]
        for s, (word, length) in enumerate(zip(words, lengths)):
            cand_ref[pl.ds(b * slots + s, 1), :] = jnp.full((1, dim), req_ref[b, s + dim // 2], jnp.int32)
            for u in range(pieces):
                units_ref[n] = word + u
                n = n + jnp.where(length > u * UNIT, 1, 0)
        return n

    count = lax.fori_loop(0, peers, listing, 0)
    for u in range(GROUP):
        units_ref[count + u] = total << slot_at

    def place(t, part, swapped):
        peer = me ^ order[t] if order else t
        first = pl.multiple_of(peer * shard + core * half, 8)
        second = pl.multiple_of(peer * shard + half - core * half, 8)
        table_ref[pl.ds(first, half), :] = part[qrows : qrows + half, :].astype(jnp.float32)
        table_ref[pl.ds(second, half), :] = swapped[...].astype(jnp.float32)
        query_ref[pl.ds(pl.multiple_of(t * qrows, 16), qrows), :] = part[:qrows, :]

    def place_loop(t, carry):
        place(t, parts[0].at[t], other_ref.at[t])
        return carry

    if order:
        for t in range(peers):
            place(t, parts[t], other_ref.at[t])
    else:
        lax.fori_loop(0, peers, place_loop, 0)

    token = lax.broadcasted_iota(jnp.int32, (UNIT, qtok), 0)
    nt = (((1,), (1,)), ((), ()))

    pair = UNIT // 2

    def fetch(g, carry):
        for j in range(FETCH):
            unit = g * FETCH + j
            word = units_ref[unit]
            base = field(word, 0, piece_bits) * (pair * passages) + field(word, piece_bits, pass_bits)
            rows = rows_ref.at[pl.ds(pl.multiple_of(unit * UNIT, UNIT), UNIT)]
            for t in range(pair):
                codes = codes_ref[base + t * passages]
                rows[t : t + 1, :] = table_ref[pl.ds(codes & 0xFFFF, 1), :]
                rows[t + pair : t + pair + 1, :] = table_ref[pl.ds(lax.shift_right_logical(codes, 16), 1), :]
        return carry

    def compare(g, carry):
        found = []
        for j in range(GROUP):
            unit = g * GROUP + j
            word = units_ref[unit]
            piece = field(word, 0, piece_bits)
            p = field(word, piece_bits, pass_bits)
            row = piece * (total + 8) + field(word, slot_at, slot_bits)
            head = lax.shift_right_logical(word, head_at)
            resid = resid_ref[p, pl.ds(pl.multiple_of(piece * UNIT, UNIT), UNIT), :]
            query = query_ref[pl.ds(pl.multiple_of(head * qtok, qtok), qtok), :]
            left = length_ref[p] - piece * UNIT
            cent = rows_ref[pl.ds(pl.multiple_of(unit * UNIT, UNIT), UNIT), :]
            v = cent + resid.astype(jnp.float32)
            both = jnp.concatenate([normalize(v).astype(jnp.bfloat16), cent.astype(jnp.bfloat16)], axis=0)
            sims = lax.dot_general(both, query, nt, preferred_element_type=jnp.float32)
            tops = [
                jnp.max(jnp.where(token < left, sims[o : o + UNIT], -1000000000.0), axis=0, keepdims=True)
                for o in (0, UNIT)
            ]
            found.append((row, tops))
        for row, (exact, approx) in found:
            best_ref[pl.ds(row, 1), :] = exact
            near_ref[pl.ds(row, 1), :] = approx
        return carry

    bring_codes.wait()
    lax.fori_loop(0, (count + FETCH - 1) // FETCH, fetch, 0)
    bring_resid.wait()
    lax.fori_loop(0, (count + GROUP - 1) // GROUP, compare, 0)

    def score(ref):
        best = ref[:total, :]
        for u in range(1, pieces):
            best = jnp.maximum(best, ref[u * (total + 8) : u * (total + 8) + total, :])
        return jnp.sum(best, axis=1, keepdims=True)

    cand = cand_ref[...]
    lane = lax.broadcasted_iota(jnp.int32, (total, dim), 1)
    placed = jnp.where(lane == cand, score(best_ref), 0.0)
    placed += jnp.where(lane == cand + q_dev * per_query, score(near_ref), 0.0)
    placed = jnp.where(cand >= 0, placed, 0.0)
    placed = jnp.sum(placed.reshape(peers, slots, dim), axis=1)
    turned = [placed] + [pltpu.roll(placed, dim - r * per_query, 1) for r in range(1, 2 * q_dev)]
    for b in range(peers):
        to = me ^ order[b] if order else b
        for r in range(2 * q_dev):
            out_ref[to, r : r + 1, :] = turned[r][b : b + 1, :]


def body(queries, cand_owner, cand_local, centroids, passage_codes, residuals, passage_lengths):
    peers = lax.axis_size("index")
    cores = lax.axis_size("query")
    q_dev, per_query = cand_owner.shape
    count = q_dev * per_query
    slots = max(2, (2 * count + peers - 1) // peers)
    seq, dim = residuals.shape[1:]
    qtok = queries.shape[1]
    qrows = q_dev * qtok
    half = centroids.shape[0] // cores
    rows = qrows + half + PAD
    order = ORDER if peers == len(ORDER) else ()
    vmem = pl.BlockSpec(memory_space=pltpu.VMEM)
    smem = pl.BlockSpec(memory_space=pltpu.SMEM)
    hbm = pl.BlockSpec(memory_space=pltpu.HBM)
    copies = 1 if order else peers
    pack_mib = 2 * copies * rows * dim * 2 // MIB
    held = [passage_codes.T, passage_lengths]
    kept = [((seq // 2, residuals.shape[0]), jnp.int32), (passage_lengths.shape, jnp.int32)]
    inputs = [cand_owner, cand_local, queries, centroids] + held
    packed, *held = pl.pallas_call(
        pack_kernel,
        out_shape=[jax.ShapeDtypeStruct((copies, rows, dim), jnp.bfloat16)]
        + [jax.ShapeDtypeStruct(*x) for x in kept],
        in_specs=[hbm] * 6,
        out_specs=[vmem] * 3,
        scratch_shapes=[
            pltpu.VMEM(passage_codes.T.shape, jnp.int32),
            pltpu.SMEM((peers,), jnp.int32),
            pltpu.VMEM((peers + PAD, dim), jnp.float32),
            pltpu.SMEM(cand_owner.shape, jnp.int32),
            pltpu.SMEM(cand_local.shape, jnp.int32),
            pltpu.VMEM(queries.shape, queries.dtype),
            pltpu.VMEM((half, dim), centroids.dtype),
            pltpu.SemaphoreType.DMA((6,)),
        ],
        compiler_params=pltpu.CompilerParams(vmem_limit_bytes=(8 + pack_mib) * MIB),
    )(*(pltpu.with_memory_space_constraint(x, pltpu.HBM) for x in inputs))
    codes, lengths = held[0].reshape(-1), held[1]
    resid = pltpu.with_memory_space_constraint(residuals, pltpu.HBM)
    if order:
        swap = lambda x, t: lax.ppermute(x, "index", [(i, i ^ t) for i in range(peers)])
        known = {0: packed[0]}
        for t in order:
            if t not in known and t not in RELAYED:
                known[t] = swap(known[0], t)
        for t in RELAYED:
            known[t] = swap(known[t ^ 1], 1)
        parts = [known[t] for t in order]
        mine = jnp.stack([part[qrows : qrows + half] for part in parts])
        asked = jnp.stack([part[qrows + half :] for part in parts])
        asked = lax.dynamic_index_in_dim(asked, lax.axis_index("index"), 1, keepdims=False)
    else:
        parts = [lax.all_to_all(packed, "index", split_axis=0, concat_axis=0, tiled=True)]
        mine = parts[0][:, qrows : qrows + half]
        asked = parts[0][:, qrows + half]
    asked = asked.astype(jnp.int32)
    piece_bits, pass_bits, slot_bits = field_bits(peers, slots, residuals.shape[0], seq)
    place = jnp.arange(peers, dtype=jnp.int32)[:, None] * slots + jnp.arange(dim // 2, dtype=jnp.int32)[None]
    head = jnp.arange(peers, dtype=jnp.int32)[:, None] * q_dev + asked[:, dim // 2 :] // per_query
    word = ((((head << slot_bits) + place) << pass_bits) + asked[:, : dim // 2]) << piece_bits
    word = jnp.where(asked[:, : dim // 2] >= 0, word, -1)
    asked = jnp.concatenate([word, asked[:, dim // 2 :]], axis=1)
    other = lax.ppermute(mine, "query", [(0, 1), (1, 0)])
    table_mib = 2 * peers * half * dim * 2 // MIB
    bests = (seq // UNIT) * (peers * slots + 8)
    scores = pl.pallas_call(
        functools.partial(score_kernel, slots, q_dev, per_query, qtok, order),
        out_shape=jax.ShapeDtypeStruct((peers, 2 * q_dev, dim), jnp.float32),
        in_specs=[smem, smem, pl.BlockSpec(memory_space=pl.ANY)] + [vmem] * (len(parts) + 1) + [hbm],
        out_specs=vmem,
        scratch_shapes=[
            pltpu.VMEM((peers * qrows, dim), jnp.bfloat16),
            pltpu.VMEM((peers * cores * half, dim), jnp.float32),
            pltpu.VMEM((peers * slots * seq + GROUP * UNIT, dim), jnp.float32),
            pltpu.VMEM((bests, qtok), jnp.float32),
            pltpu.VMEM((bests, qtok), jnp.float32),
            pltpu.VMEM((peers * slots, dim), jnp.int32),
            pltpu.SMEM((peers * slots * (seq // UNIT) + GROUP,), jnp.int32),
            pltpu.SMEM(codes.shape, jnp.int32),
            pltpu.VMEM(residuals.shape, residuals.dtype),
            pltpu.SemaphoreType.DMA((2,)),
        ],
        compiler_params=pltpu.CompilerParams(vmem_limit_bytes=(12 + 4 * table_mib + peers * slots * seq * dim * 4 // MIB) * MIB),
    )(asked, lengths, codes, *parts, other, resid)
    back = lax.all_to_all(scores, "index", split_axis=0, concat_axis=0, tiled=True)
    result = jnp.sum(back[:, :, :per_query], axis=0)
    return result[:q_dev], result[q_dev:]


def solution(mesh):
    in_specs = (
        P(("group", "index", "query"), None, None),
        P(("group", "index", "query"), None),
        P(("group", "index", "query"), None),
        P("index", None),
        P("index", None),
        P("index", None, None),
        P("index"),
    )
    out_specs = (P(("group", "index", "query"), None), P(("group", "index", "query"), None))
    return jax.shard_map(body, mesh=mesh, in_specs=in_specs, out_specs=out_specs, check_vma=False)
```

```python
import functools

import jax
import jax.numpy as jnp
from jax import lax
from jax.experimental import pallas as pl
from jax.experimental.pallas import tpu as pltpu
from jax.sharding import PartitionSpec as P

EPS = 1e-06
PAD = 16
UNIT = 32
GROUP = 32
ORDER = (4, 6, 1, 3, 2, 5, 7, 0)
RELAYED = (5, 7)
FETCH = 8
MIB = 1024 * 1024


def normalize(wide):
    return wide * lax.rsqrt(jnp.sum(wide * wide, axis=-1, keepdims=True) + EPS)


def pack_kernel(
    owner_hbm,
    local_hbm,
    queries_hbm,
    cent_hbm,
    codes_hbm,
    length_hbm,
    out_ref,
    codes_out,
    length_out,
    codes_ref,
    count_ref,
    req_ref,
    owner_ref,
    local_ref,
    queries_ref,
    cent_ref,
    sems,
):
    copies = out_ref.shape[0]
    peers = count_ref.shape[0]
    q_dev, per_query = owner_ref.shape
    qrows = queries_ref.shape[0] * queries_ref.shape[1]
    half, dim = cent_ref.shape
    core = lax.axis_index("query")
    cent_half = cent_hbm.at[pl.ds(pl.multiple_of(core * half, 16), half)]
    moves = [
        pltpu.make_async_copy(src, dst, sems.at[i])
        for i, (src, dst) in enumerate(
            (
                (owner_hbm, owner_ref),
                (local_hbm, local_ref),
                (queries_hbm, queries_ref),
                (cent_half, cent_ref),
                (codes_hbm, codes_ref),
                (length_hbm, length_out),
            )
        )
    ]
    for move in moves:
        move.start()

    def clear(i, carry):
        count_ref[i] = 0
        return carry

    lax.fori_loop(0, peers, clear, 0)
    for move in moves[:4]:
        move.wait()
    row = lax.broadcasted_iota(jnp.int32, req_ref.shape, 0)
    lane = lax.broadcasted_iota(jnp.int32, req_ref.shape, 1)
    req = jnp.full(req_ref.shape, -1, jnp.int32)
    for q in range(q_dev):
        for k in range(per_query):
            owner = owner_ref[q, k]
            slot = count_ref[owner]
            count_ref[owner] = slot + 1
            here = row == owner
            req = jnp.where(here & (lane == slot), local_ref[q, k], req)
            req = jnp.where(here & (lane == slot + dim // 2), q * per_query + k, req)
    req_ref[...] = req.astype(jnp.float32)
    qnorm = normalize(queries_ref[...].reshape(qrows, dim).astype(jnp.float32)).astype(jnp.bfloat16)

    def send(d, carry):
        out_ref[d, :qrows, :] = qnorm
        out_ref[d, qrows : qrows + half, :] = cent_ref[...]
        asked = req_ref[pl.ds(d, PAD), :]
        out_ref[d, qrows + half :, :] = asked.astype(jnp.bfloat16)
        return carry

    lax.fori_loop(0, copies, send, 0)
    for move in moves[4:]:
        move.wait()
    pair = UNIT // 2
    for u in range(codes_ref.shape[0] // UNIT):
        low = codes_ref[u * UNIT : u * UNIT + pair, :]
        high = codes_ref[u * UNIT + pair : (u + 1) * UNIT, :]
        codes_out[u * pair : (u + 1) * pair, :] = low | (high << 16)


def field_bits(peers, slots, passages, seq):
    return (seq // UNIT - 1).bit_length(), (passages - 1).bit_length(), (peers * slots).bit_length()


def score_kernel(slots, q_dev, per_query, qtok, order, req_any, length_any, codes_any, *refs):
    (*parts, other_ref, resid_hbm, out_ref) = refs[:-12]
    query_ref, table_ref, rows_ref, best_ref, near_ref, cand_ref, units_ref = refs[-12:-5]
    req_ref, length_ref, codes_ref, resid_ref, sems = refs[-5:]
    peers, half, dim = other_ref.shape
    qrows = q_dev * qtok
    passages, seq = resid_hbm.shape[:2]
    pieces = seq // UNIT
    shard = 2 * half
    total = peers * slots
    me = lax.axis_index("index")
    core = lax.axis_index("query")

    bring_req = pltpu.make_async_copy(req_any, req_ref, sems.at[0])
    bring_length = pltpu.make_async_copy(length_any, length_ref, sems.at[1])
    bring_codes = pltpu.make_async_copy(codes_any, codes_ref, sems.at[2])
    bring_resid = pltpu.make_async_copy(resid_hbm, resid_ref, sems.at[3])
    for bring in (bring_req, bring_length, bring_codes, bring_resid):
        bring.start()
    best_ref[...] = jnp.full(best_ref.shape, -1000000000.0, jnp.float32)
    near_ref[...] = jnp.full(near_ref.shape, -1000000000.0, jnp.float32)

    piece_bits, pass_bits, slot_bits = field_bits(peers, slots, passages, seq)
    cand_bits = (per_query - 1).bit_length()
    slot_at = piece_bits + pass_bits
    head_at = slot_at + slot_bits

    def field(word, at, bits):
        return lax.shift_right_logical(word, at) & ((1 << bits) - 1)

    def listing(b, n):
        words = [req_ref[b, s] for s in range(slots)]
        lengths = [jnp.where(w >= 0, length_ref[field(w, piece_bits, pass_bits)], 0) for w in words]
        for s, (word, length) in enumerate(zip(words, lengths)):
            cand_ref[pl.ds(b * slots + s, 1), :] = jnp.full((1, dim), req_ref[b, s + dim // 2], jnp.int32)
            for u in range(pieces):
                units_ref[n] = word + u
                n = n + jnp.where(length > u * UNIT, 1, 0)
        return n

    def place(t, part, swapped):
        peer = me ^ order[t] if order else t
        first = pl.multiple_of(peer * shard + core * half, 8)
        second = pl.multiple_of(peer * shard + half - core * half, 8)
        table_ref[pl.ds(first, half), :] = part[qrows : qrows + half, :].astype(jnp.float32)
        table_ref[pl.ds(second, half), :] = swapped[...].astype(jnp.float32)
        query_ref[pl.ds(pl.multiple_of(t * qrows, 16), qrows), :] = part[:qrows, :]

    def place_loop(t, carry):
        place(t, parts[0].at[t], other_ref.at[t])
        return carry

    if order:
        for t in range(peers):
            place(t, parts[t], other_ref.at[t])
    else:
        lax.fori_loop(0, peers, place_loop, 0)

    bring_req.wait()
    bring_length.wait()
    count = lax.fori_loop(0, peers, listing, 0)
    for u in range(GROUP):
        units_ref[count + u] = total << slot_at

    token = lax.broadcasted_iota(jnp.int32, (UNIT, qtok), 0)
    nt = (((1,), (1,)), ((), ()))

    pair = UNIT // 2

    def fetch(g, carry):
        for j in range(FETCH):
            unit = g * FETCH + j
            word = units_ref[unit]
            base = field(word, 0, piece_bits) * (pair * passages) + field(word, piece_bits, pass_bits)
            rows = rows_ref.at[pl.ds(pl.multiple_of(unit * UNIT, UNIT), UNIT)]
            for t in range(pair):
                codes = codes_ref[base + t * passages]
                rows[t : t + 1, :] = table_ref[pl.ds(codes & 0xFFFF, 1), :]
                rows[t + pair : t + pair + 1, :] = table_ref[pl.ds(lax.shift_right_logical(codes, 16), 1), :]
        return carry

    def compare(g, carry):
        found = []
        for j in range(GROUP):
            unit = g * GROUP + j
            word = units_ref[unit]
            piece = field(word, 0, piece_bits)
            p = field(word, piece_bits, pass_bits)
            row = piece * (total + 8) + field(word, slot_at, slot_bits)
            head = lax.shift_right_logical(word, head_at)
            resid = resid_ref[p, pl.ds(pl.multiple_of(piece * UNIT, UNIT), UNIT), :]
            query = query_ref[pl.ds(pl.multiple_of(head * qtok, qtok), qtok), :]
            left = length_ref[p] - piece * UNIT
            cent = rows_ref[pl.ds(pl.multiple_of(unit * UNIT, UNIT), UNIT), :]
            v = cent + resid.astype(jnp.float32)
            both = jnp.concatenate([normalize(v).astype(jnp.bfloat16), cent.astype(jnp.bfloat16)], axis=0)
            sims = lax.dot_general(both, query, nt, preferred_element_type=jnp.float32)
            tops = [
                jnp.max(jnp.where(token < left, sims[o : o + UNIT], -1000000000.0), axis=0, keepdims=True)
                for o in (0, UNIT)
            ]
            found.append((row, tops))
        for row, (exact, approx) in found:
            best_ref[pl.ds(row, 1), :] = exact
            near_ref[pl.ds(row, 1), :] = approx
        return carry

    bring_codes.wait()
    lax.fori_loop(0, (count + FETCH - 1) // FETCH, fetch, 0)
    bring_resid.wait()
    lax.fori_loop(0, (count + GROUP - 1) // GROUP, compare, 0)

    def score(ref):
        best = ref[:total, :]
        for u in range(1, pieces):
            best = jnp.maximum(best, ref[u * (total + 8) : u * (total + 8) + total, :])
        return jnp.sum(best, axis=1, keepdims=True)

    cand = cand_ref[...]
    lane = lax.broadcasted_iota(jnp.int32, (total, dim), 1)
    placed = jnp.where(lane == cand, score(best_ref), 0.0)
    placed += jnp.where(lane == cand + q_dev * per_query, score(near_ref), 0.0)
    placed = jnp.where(cand >= 0, placed, 0.0)
    placed = jnp.sum(placed.reshape(peers, slots, dim), axis=1)
    turned = [placed] + [pltpu.roll(placed, dim - r * per_query, 1) for r in range(1, 2 * q_dev)]
    for b in range(peers):
        to = me ^ order[b] if order else b
        for r in range(2 * q_dev):
            out_ref[to, r : r + 1, :] = turned[r][b : b + 1, :]


def body(queries, cand_owner, cand_local, centroids, passage_codes, residuals, passage_lengths):
    peers = lax.axis_size("index")
    cores = lax.axis_size("query")
    q_dev, per_query = cand_owner.shape
    count = q_dev * per_query
    slots = max(2, (2 * count + peers - 1) // peers)
    seq, dim = residuals.shape[1:]
    qtok = queries.shape[1]
    qrows = q_dev * qtok
    half = centroids.shape[0] // cores
    rows = qrows + half + PAD
    order = ORDER if peers == len(ORDER) else ()
    vmem = pl.BlockSpec(memory_space=pltpu.VMEM)
    smem = pl.BlockSpec(memory_space=pltpu.SMEM)
    hbm = pl.BlockSpec(memory_space=pltpu.HBM)
    copies = 1 if order else peers
    pack_mib = 2 * copies * rows * dim * 2 // MIB
    held = [passage_codes.T, passage_lengths]
    kept = [((seq // 2, residuals.shape[0]), jnp.int32), (passage_lengths.shape, jnp.int32)]
    inputs = [cand_owner, cand_local, queries, centroids] + held
    packed, *held = pl.pallas_call(
        pack_kernel,
        out_shape=[jax.ShapeDtypeStruct((copies, rows, dim), jnp.bfloat16)]
        + [jax.ShapeDtypeStruct(*x) for x in kept],
        in_specs=[hbm] * 6,
        out_specs=[vmem] * 3,
        scratch_shapes=[
            pltpu.VMEM(passage_codes.T.shape, jnp.int32),
            pltpu.SMEM((peers,), jnp.int32),
            pltpu.VMEM((peers + PAD, dim), jnp.float32),
            pltpu.SMEM(cand_owner.shape, jnp.int32),
            pltpu.SMEM(cand_local.shape, jnp.int32),
            pltpu.VMEM(queries.shape, queries.dtype),
            pltpu.VMEM((half, dim), centroids.dtype),
            pltpu.SemaphoreType.DMA((6,)),
        ],
        compiler_params=pltpu.CompilerParams(vmem_limit_bytes=(8 + pack_mib) * MIB),
    )(*(pltpu.with_memory_space_constraint(x, pltpu.HBM) for x in inputs))
    codes, lengths = held[0].reshape(-1), held[1]
    resid = pltpu.with_memory_space_constraint(residuals, pltpu.HBM)
    if order:
        swap = lambda x, t: lax.ppermute(x, "index", [(i, i ^ t) for i in range(peers)])
        known = {0: packed[0]}
        for t in order:
            if t not in known and t not in RELAYED:
                known[t] = swap(known[0], t)
        for t in RELAYED:
            known[t] = swap(known[t ^ 1], 1)
        parts = [known[t] for t in order]
        mine = jnp.stack([part[qrows : qrows + half] for part in parts])
        asked = jnp.stack([part[qrows + half :] for part in parts])
        asked = lax.dynamic_index_in_dim(asked, lax.axis_index("index"), 1, keepdims=False)
    else:
        parts = [lax.all_to_all(packed, "index", split_axis=0, concat_axis=0, tiled=True)]
        mine = parts[0][:, qrows : qrows + half]
        asked = parts[0][:, qrows + half]
    asked = asked.astype(jnp.int32)
    piece_bits, pass_bits, slot_bits = field_bits(peers, slots, residuals.shape[0], seq)
    place = jnp.arange(peers, dtype=jnp.int32)[:, None] * slots + jnp.arange(dim // 2, dtype=jnp.int32)[None]
    head = jnp.arange(peers, dtype=jnp.int32)[:, None] * q_dev + asked[:, dim // 2 :] // per_query
    word = ((((head << slot_bits) + place) << pass_bits) + asked[:, : dim // 2]) << piece_bits
    word = jnp.where(asked[:, : dim // 2] >= 0, word, -1)
    asked = jnp.concatenate([word, asked[:, dim // 2 :]], axis=1)
    other = lax.ppermute(mine, "query", [(0, 1), (1, 0)])
    table_mib = 2 * peers * half * dim * 2 // MIB
    bests = (seq // UNIT) * (peers * slots + 8)
    scores = pl.pallas_call(
        functools.partial(score_kernel, slots, q_dev, per_query, qtok, order),
        out_shape=jax.ShapeDtypeStruct((peers, 2 * q_dev, dim), jnp.float32),
        in_specs=[pl.BlockSpec(memory_space=pl.ANY)] * 3 + [vmem] * (len(parts) + 1) + [hbm],
        out_specs=vmem,
        scratch_shapes=[
            pltpu.VMEM((peers * qrows, dim), jnp.bfloat16),
            pltpu.VMEM((peers * cores * half, dim), jnp.float32),
            pltpu.VMEM((peers * slots * seq + GROUP * UNIT, dim), jnp.float32),
            pltpu.VMEM((bests, qtok), jnp.float32),
            pltpu.VMEM((bests, qtok), jnp.float32),
            pltpu.VMEM((peers * slots, dim), jnp.int32),
            pltpu.SMEM((peers * slots * (seq // UNIT) + GROUP,), jnp.int32),
            pltpu.SMEM(asked.shape, jnp.int32),
            pltpu.SMEM(lengths.shape, jnp.int32),
            pltpu.SMEM(codes.shape, jnp.int32),
            pltpu.VMEM(residuals.shape, residuals.dtype),
            pltpu.SemaphoreType.DMA((4,)),
        ],
        compiler_params=pltpu.CompilerParams(vmem_limit_bytes=(12 + 4 * table_mib + peers * slots * seq * dim * 4 // MIB) * MIB),
    )(asked, lengths, codes, *parts, other, resid)
    back = lax.all_to_all(scores, "index", split_axis=0, concat_axis=0, tiled=True)
    result = jnp.sum(back[:, :, :per_query], axis=0)
    return result[:q_dev], result[q_dev:]


def solution(mesh):
    in_specs = (
        P(("group", "index", "query"), None, None),
        P(("group", "index", "query"), None),
        P(("group", "index", "query"), None),
        P("index", None),
        P("index", None),
        P("index", None, None),
        P("index"),
    )
    out_specs = (P(("group", "index", "query"), None), P(("group", "index", "query"), None))
    return jax.shard_map(body, mesh=mesh, in_specs=in_specs, out_specs=out_specs, check_vma=False)
```

```python
import functools

import jax
import jax.numpy as jnp
from jax import lax
from jax.experimental import pallas as pl
from jax.experimental.pallas import tpu as pltpu
from jax.sharding import PartitionSpec as P

EPS = 1e-06
PAD = 16
UNIT = 32
GROUP = 32
ORDER = (4, 6, 1, 3, 2, 5, 7, 0)
RELAYED = (5, 7)
FETCH = 8
MIB = 1024 * 1024


def normalize(wide):
    return wide * lax.rsqrt(jnp.sum(wide * wide, axis=-1, keepdims=True) + EPS)


def pack_kernel(
    owner_hbm,
    local_hbm,
    queries_hbm,
    cent_hbm,
    codes_hbm,
    length_hbm,
    out_ref,
    codes_out,
    length_out,
    codes_ref,
    count_ref,
    req_ref,
    owner_ref,
    local_ref,
    queries_ref,
    cent_ref,
    sems,
):
    copies = out_ref.shape[0]
    peers = count_ref.shape[0]
    q_dev, per_query = owner_ref.shape
    qrows = queries_ref.shape[0] * queries_ref.shape[1]
    half, dim = cent_ref.shape
    core = lax.axis_index("query")
    cent_half = cent_hbm.at[pl.ds(pl.multiple_of(core * half, 16), half)]
    moves = [
        pltpu.make_async_copy(src, dst, sems.at[i])
        for i, (src, dst) in enumerate(
            (
                (owner_hbm, owner_ref),
                (local_hbm, local_ref),
                (queries_hbm, queries_ref),
                (cent_half, cent_ref),
                (codes_hbm, codes_ref),
                (length_hbm, length_out),
            )
        )
    ]
    for move in moves:
        move.start()

    def clear(i, carry):
        count_ref[i] = 0
        return carry

    lax.fori_loop(0, peers, clear, 0)
    for move in moves[:4]:
        move.wait()
    row = lax.broadcasted_iota(jnp.int32, req_ref.shape, 0)
    lane = lax.broadcasted_iota(jnp.int32, req_ref.shape, 1)
    req = jnp.full(req_ref.shape, -1, jnp.int32)
    for q in range(q_dev):
        for k in range(per_query):
            owner = owner_ref[q, k]
            slot = count_ref[owner]
            count_ref[owner] = slot + 1
            here = row == owner
            req = jnp.where(here & (lane == slot), local_ref[q, k], req)
            req = jnp.where(here & (lane == slot + dim // 2), q * per_query + k, req)
    req_ref[...] = req.astype(jnp.float32)
    qnorm = normalize(queries_ref[...].reshape(qrows, dim).astype(jnp.float32)).astype(jnp.bfloat16)

    def send(d, carry):
        out_ref[d, :qrows, :] = qnorm
        out_ref[d, qrows : qrows + half, :] = cent_ref[...]
        asked = req_ref[pl.ds(d, PAD), :]
        out_ref[d, qrows + half :, :] = asked.astype(jnp.bfloat16)
        return carry

    lax.fori_loop(0, copies, send, 0)
    for move in moves[4:]:
        move.wait()
    pair = UNIT // 2
    for u in range(codes_ref.shape[0] // UNIT):
        low = codes_ref[u * UNIT : u * UNIT + pair, :]
        high = codes_ref[u * UNIT + pair : (u + 1) * UNIT, :]
        codes_out[u * pair : (u + 1) * pair, :] = low | (high << 16)


def field_bits(peers, slots, passages, seq):
    return (seq // UNIT - 1).bit_length(), (passages - 1).bit_length(), (peers * slots).bit_length()


def score_kernel(slots, q_dev, per_query, qtok, order, req_any, length_any, codes_any, *refs):
    (*parts, other_ref, resid_hbm, out_ref) = refs[:-12]
    query_ref, table_ref, rows_ref, best_ref, near_ref, cand_ref, units_ref = refs[-12:-5]
    req_ref, length_ref, codes_ref, resid_ref, sems = refs[-5:]
    peers, half, dim = other_ref.shape
    qrows = q_dev * qtok
    passages, seq = resid_hbm.shape[:2]
    pieces = seq // UNIT
    shard = 2 * half
    total = peers * slots
    me = lax.axis_index("index")
    core = lax.axis_index("query")

    bring_req = pltpu.make_async_copy(req_any, req_ref, sems.at[0])
    bring_length = pltpu.make_async_copy(length_any, length_ref, sems.at[1])
    bring_codes = pltpu.make_async_copy(codes_any, codes_ref, sems.at[2])
    bring_resid = pltpu.make_async_copy(resid_hbm, resid_ref, sems.at[3])
    for bring in (bring_req, bring_length, bring_codes, bring_resid):
        bring.start()
    best_ref[...] = jnp.full(best_ref.shape, -1000000000.0, jnp.float32)
    near_ref[...] = jnp.full(near_ref.shape, -1000000000.0, jnp.float32)

    piece_bits, pass_bits, slot_bits = field_bits(peers, slots, passages, seq)
    cand_bits = (per_query - 1).bit_length()
    slot_at = piece_bits + pass_bits
    head_at = slot_at + slot_bits

    def field(word, at, bits):
        return lax.shift_right_logical(word, at) & ((1 << bits) - 1)

    def listing(b, n):
        words = [req_ref[b, s] for s in range(slots)]
        lengths = [jnp.where(w >= 0, length_ref[field(w, piece_bits, pass_bits)], 0) for w in words]
        for s, (word, length) in enumerate(zip(words, lengths)):
            cand_ref[pl.ds(b * slots + s, 1), :] = jnp.full((1, dim), req_ref[b, s + dim // 2], jnp.int32)
            for u in range(pieces):
                units_ref[n] = word + u
                n = n + jnp.where(length > u * UNIT, 1, 0)
        return n

    def place(t, part, swapped):
        peer = me ^ order[t] if order else t
        first = pl.multiple_of(peer * shard + core * half, 8)
        second = pl.multiple_of(peer * shard + half - core * half, 8)
        table_ref[pl.ds(first, half), :] = part[qrows : qrows + half, :].astype(jnp.float32)
        table_ref[pl.ds(second, half), :] = swapped[...].astype(jnp.float32)
        query_ref[pl.ds(pl.multiple_of(t * qrows, 16), qrows), :] = part[:qrows, :]

    def place_loop(t, carry):
        place(t, parts[0].at[t], other_ref.at[t])
        return carry

    if order:
        for t in range(peers):
            place(t, parts[t], other_ref.at[t])
    else:
        lax.fori_loop(0, peers, place_loop, 0)

    bring_req.wait()
    bring_length.wait()
    count = lax.fori_loop(0, peers, listing, 0, unroll=peers <= PAD)
    for u in range(GROUP):
        units_ref[count + u] = total << slot_at

    token = lax.broadcasted_iota(jnp.int32, (UNIT, qtok), 0)
    nt = (((1,), (1,)), ((), ()))

    pair = UNIT // 2

    def fetch(g, carry):
        for j in range(FETCH):
            unit = g * FETCH + j
            word = units_ref[unit]
            base = field(word, 0, piece_bits) * (pair * passages) + field(word, piece_bits, pass_bits)
            rows = rows_ref.at[pl.ds(pl.multiple_of(unit * UNIT, UNIT), UNIT)]
            for t in range(pair):
                codes = codes_ref[base + t * passages]
                rows[t : t + 1, :] = table_ref[pl.ds(codes & 0xFFFF, 1), :]
                rows[t + pair : t + pair + 1, :] = table_ref[pl.ds(lax.shift_right_logical(codes, 16), 1), :]
        return carry

    def compare(g, carry):
        found = []
        for j in range(GROUP):
            unit = g * GROUP + j
            word = units_ref[unit]
            piece = field(word, 0, piece_bits)
            p = field(word, piece_bits, pass_bits)
            row = piece * (total + 8) + field(word, slot_at, slot_bits)
            head = lax.shift_right_logical(word, head_at)
            resid = resid_ref[p, pl.ds(pl.multiple_of(piece * UNIT, UNIT), UNIT), :]
            query = query_ref[pl.ds(pl.multiple_of(head * qtok, qtok), qtok), :]
            left = length_ref[p] - piece * UNIT
            cent = rows_ref[pl.ds(pl.multiple_of(unit * UNIT, UNIT), UNIT), :]
            v = cent + resid.astype(jnp.float32)
            both = jnp.concatenate([normalize(v).astype(jnp.bfloat16), cent.astype(jnp.bfloat16)], axis=0)
            sims = lax.dot_general(both, query, nt, preferred_element_type=jnp.float32)
            tops = [
                jnp.max(jnp.where(token < left, sims[o : o + UNIT], -1000000000.0), axis=0, keepdims=True)
                for o in (0, UNIT)
            ]
            found.append((row, tops))
        for row, (exact, approx) in found:
            best_ref[pl.ds(row, 1), :] = exact
            near_ref[pl.ds(row, 1), :] = approx
        return carry

    bring_codes.wait()
    lax.fori_loop(0, (count + FETCH - 1) // FETCH, fetch, 0)
    bring_resid.wait()
    lax.fori_loop(0, (count + GROUP - 1) // GROUP, compare, 0)

    def score(ref):
        best = ref[:total, :]
        for u in range(1, pieces):
            best = jnp.maximum(best, ref[u * (total + 8) : u * (total + 8) + total, :])
        return jnp.sum(best, axis=1, keepdims=True)

    cand = cand_ref[...]
    lane = lax.broadcasted_iota(jnp.int32, (total, dim), 1)
    placed = jnp.where(lane == cand, score(best_ref), 0.0)
    placed += jnp.where(lane == cand + q_dev * per_query, score(near_ref), 0.0)
    placed = jnp.where(cand >= 0, placed, 0.0)
    placed = jnp.sum(placed.reshape(peers, slots, dim), axis=1)
    turned = [placed] + [pltpu.roll(placed, dim - r * per_query, 1) for r in range(1, 2 * q_dev)]
    for b in range(peers):
        to = me ^ order[b] if order else b
        for r in range(2 * q_dev):
            out_ref[to, r : r + 1, :] = turned[r][b : b + 1, :]


def body(queries, cand_owner, cand_local, centroids, passage_codes, residuals, passage_lengths):
    peers = lax.axis_size("index")
    cores = lax.axis_size("query")
    q_dev, per_query = cand_owner.shape
    count = q_dev * per_query
    slots = max(2, (2 * count + peers - 1) // peers)
    seq, dim = residuals.shape[1:]
    qtok = queries.shape[1]
    qrows = q_dev * qtok
    half = centroids.shape[0] // cores
    rows = qrows + half + PAD
    order = ORDER if peers == len(ORDER) else ()
    vmem = pl.BlockSpec(memory_space=pltpu.VMEM)
    smem = pl.BlockSpec(memory_space=pltpu.SMEM)
    hbm = pl.BlockSpec(memory_space=pltpu.HBM)
    copies = 1 if order else peers
    pack_mib = 2 * copies * rows * dim * 2 // MIB
    held = [passage_codes.T, passage_lengths]
    kept = [((seq // 2, residuals.shape[0]), jnp.int32), (passage_lengths.shape, jnp.int32)]
    inputs = [cand_owner, cand_local, queries, centroids] + held
    packed, *held = pl.pallas_call(
        pack_kernel,
        out_shape=[jax.ShapeDtypeStruct((copies, rows, dim), jnp.bfloat16)]
        + [jax.ShapeDtypeStruct(*x) for x in kept],
        in_specs=[hbm] * 6,
        out_specs=[vmem] * 3,
        scratch_shapes=[
            pltpu.VMEM(passage_codes.T.shape, jnp.int32),
            pltpu.SMEM((peers,), jnp.int32),
            pltpu.VMEM((peers + PAD, dim), jnp.float32),
            pltpu.SMEM(cand_owner.shape, jnp.int32),
            pltpu.SMEM(cand_local.shape, jnp.int32),
            pltpu.VMEM(queries.shape, queries.dtype),
            pltpu.VMEM((half, dim), centroids.dtype),
            pltpu.SemaphoreType.DMA((6,)),
        ],
        compiler_params=pltpu.CompilerParams(vmem_limit_bytes=(8 + pack_mib) * MIB),
    )(*(pltpu.with_memory_space_constraint(x, pltpu.HBM) for x in inputs))
    codes, lengths = held[0].reshape(-1), held[1]
    resid = pltpu.with_memory_space_constraint(residuals, pltpu.HBM)
    if order:
        swap = lambda x, t: lax.ppermute(x, "index", [(i, i ^ t) for i in range(peers)])
        known = {0: packed[0]}
        for t in order:
            if t not in known and t not in RELAYED:
                known[t] = swap(known[0], t)
        for t in RELAYED:
            known[t] = swap(known[t ^ 1], 1)
        parts = [known[t] for t in order]
        mine = jnp.stack([part[qrows : qrows + half] for part in parts])
        asked = jnp.stack([part[qrows + half :] for part in parts])
        asked = lax.dynamic_index_in_dim(asked, lax.axis_index("index"), 1, keepdims=False)
    else:
        parts = [lax.all_to_all(packed, "index", split_axis=0, concat_axis=0, tiled=True)]
        mine = parts[0][:, qrows : qrows + half]
        asked = parts[0][:, qrows + half]
    asked = asked.astype(jnp.int32)
    piece_bits, pass_bits, slot_bits = field_bits(peers, slots, residuals.shape[0], seq)
    place = jnp.arange(peers, dtype=jnp.int32)[:, None] * slots + jnp.arange(dim // 2, dtype=jnp.int32)[None]
    head = jnp.arange(peers, dtype=jnp.int32)[:, None] * q_dev + asked[:, dim // 2 :] // per_query
    word = ((((head << slot_bits) + place) << pass_bits) + asked[:, : dim // 2]) << piece_bits
    word = jnp.where(asked[:, : dim // 2] >= 0, word, -1)
    asked = jnp.concatenate([word, asked[:, dim // 2 :]], axis=1)
    other = lax.ppermute(mine, "query", [(0, 1), (1, 0)])
    table_mib = 2 * peers * half * dim * 2 // MIB
    bests = (seq // UNIT) * (peers * slots + 8)
    scores = pl.pallas_call(
        functools.partial(score_kernel, slots, q_dev, per_query, qtok, order),
        out_shape=jax.ShapeDtypeStruct((peers, 2 * q_dev, dim), jnp.float32),
        in_specs=[pl.BlockSpec(memory_space=pl.ANY)] * 3 + [vmem] * (len(parts) + 1) + [hbm],
        out_specs=vmem,
        scratch_shapes=[
            pltpu.VMEM((peers * qrows, dim), jnp.bfloat16),
            pltpu.VMEM((peers * cores * half, dim), jnp.float32),
            pltpu.VMEM((peers * slots * seq + GROUP * UNIT, dim), jnp.float32),
            pltpu.VMEM((bests, qtok), jnp.float32),
            pltpu.VMEM((bests, qtok), jnp.float32),
            pltpu.VMEM((peers * slots, dim), jnp.int32),
            pltpu.SMEM((peers * slots * (seq // UNIT) + GROUP,), jnp.int32),
            pltpu.SMEM(asked.shape, jnp.int32),
            pltpu.SMEM(lengths.shape, jnp.int32),
            pltpu.SMEM(codes.shape, jnp.int32),
            pltpu.VMEM(residuals.shape, residuals.dtype),
            pltpu.SemaphoreType.DMA((4,)),
        ],
        compiler_params=pltpu.CompilerParams(vmem_limit_bytes=(12 + 4 * table_mib + peers * slots * seq * dim * 4 // MIB) * MIB),
    )(asked, lengths, codes, *parts, other, resid)
    back = lax.all_to_all(scores, "index", split_axis=0, concat_axis=0, tiled=True)
    result = jnp.sum(back[:, :, :per_query], axis=0)
    return result[:q_dev], result[q_dev:]


def solution(mesh):
    in_specs = (
        P(("group", "index", "query"), None, None),
        P(("group", "index", "query"), None),
        P(("group", "index", "query"), None),
        P("index", None),
        P("index", None),
        P("index", None, None),
        P("index"),
    )
    out_specs = (P(("group", "index", "query"), None), P(("group", "index", "query"), None))
    return jax.shard_map(body, mesh=mesh, in_specs=in_specs, out_specs=out_specs, check_vma=False)
```

```python
import functools

import jax
import jax.numpy as jnp
from jax import lax
from jax.experimental import pallas as pl
from jax.experimental.pallas import tpu as pltpu
from jax.sharding import PartitionSpec as P

EPS = 1e-06
PAD = 16
UNIT = 32
GROUP = 32
ORDER = (4, 6, 1, 2, 3, 5, 7, 0)
RELAYED = (5, 7)
FETCH = 8
MIB = 1024 * 1024


def normalize(wide):
    return wide * lax.rsqrt(jnp.sum(wide * wide, axis=-1, keepdims=True) + EPS)


def pack_kernel(
    owner_hbm,
    local_hbm,
    queries_hbm,
    cent_hbm,
    codes_hbm,
    length_hbm,
    out_ref,
    codes_out,
    length_out,
    codes_ref,
    count_ref,
    req_ref,
    owner_ref,
    local_ref,
    queries_ref,
    cent_ref,
    sems,
):
    copies = out_ref.shape[0]
    peers = count_ref.shape[0]
    q_dev, per_query = owner_ref.shape
    qrows = queries_ref.shape[0] * queries_ref.shape[1]
    half, dim = cent_ref.shape
    core = lax.axis_index("query")
    cent_half = cent_hbm.at[pl.ds(pl.multiple_of(core * half, 16), half)]
    moves = [
        pltpu.make_async_copy(src, dst, sems.at[i])
        for i, (src, dst) in enumerate(
            (
                (owner_hbm, owner_ref),
                (local_hbm, local_ref),
                (queries_hbm, queries_ref),
                (cent_half, cent_ref),
                (codes_hbm, codes_ref),
                (length_hbm, length_out),
            )
        )
    ]
    for move in moves:
        move.start()

    def clear(i, carry):
        count_ref[i] = 0
        return carry

    lax.fori_loop(0, peers, clear, 0)
    for move in moves[:4]:
        move.wait()
    row = lax.broadcasted_iota(jnp.int32, req_ref.shape, 0)
    lane = lax.broadcasted_iota(jnp.int32, req_ref.shape, 1)
    req = jnp.full(req_ref.shape, -1, jnp.int32)
    for q in range(q_dev):
        for k in range(per_query):
            owner = owner_ref[q, k]
            slot = count_ref[owner]
            count_ref[owner] = slot + 1
            here = row == owner
            req = jnp.where(here & (lane == slot), local_ref[q, k], req)
            req = jnp.where(here & (lane == slot + dim // 2), q * per_query + k, req)
    req_ref[...] = req.astype(jnp.float32)
    qnorm = normalize(queries_ref[...].reshape(qrows, dim).astype(jnp.float32)).astype(jnp.bfloat16)

    def send(d, carry):
        out_ref[d, :qrows, :] = qnorm
        out_ref[d, qrows : qrows + half, :] = cent_ref[...]
        asked = req_ref[pl.ds(d, PAD), :]
        out_ref[d, qrows + half :, :] = asked.astype(jnp.bfloat16)
        return carry

    lax.fori_loop(0, copies, send, 0)
    for move in moves[4:]:
        move.wait()
    pair = UNIT // 2
    for u in range(codes_ref.shape[0] // UNIT):
        low = codes_ref[u * UNIT : u * UNIT + pair, :]
        high = codes_ref[u * UNIT + pair : (u + 1) * UNIT, :]
        codes_out[u * pair : (u + 1) * pair, :] = low | (high << 16)


def field_bits(peers, slots, passages, seq):
    return (seq // UNIT - 1).bit_length(), (passages - 1).bit_length(), (peers * slots).bit_length()


def score_kernel(slots, q_dev, per_query, qtok, order, req_any, length_any, codes_any, *refs):
    (*parts, other_ref, resid_hbm, out_ref) = refs[:-12]
    query_ref, table_ref, rows_ref, best_ref, near_ref, cand_ref, units_ref = refs[-12:-5]
    req_ref, length_ref, codes_ref, resid_ref, sems = refs[-5:]
    peers, half, dim = other_ref.shape
    qrows = q_dev * qtok
    passages, seq = resid_hbm.shape[:2]
    pieces = seq // UNIT
    shard = 2 * half
    total = peers * slots
    me = lax.axis_index("index")
    core = lax.axis_index("query")

    bring_req = pltpu.make_async_copy(req_any, req_ref, sems.at[0])
    bring_length = pltpu.make_async_copy(length_any, length_ref, sems.at[1])
    bring_codes = pltpu.make_async_copy(codes_any, codes_ref, sems.at[2])
    bring_resid = pltpu.make_async_copy(resid_hbm, resid_ref, sems.at[3])
    for bring in (bring_req, bring_length, bring_codes, bring_resid):
        bring.start()
    best_ref[...] = jnp.full(best_ref.shape, -1000000000.0, jnp.float32)
    near_ref[...] = jnp.full(near_ref.shape, -1000000000.0, jnp.float32)

    piece_bits, pass_bits, slot_bits = field_bits(peers, slots, passages, seq)
    cand_bits = (per_query - 1).bit_length()
    slot_at = piece_bits + pass_bits
    head_at = slot_at + slot_bits

    def field(word, at, bits):
        return lax.shift_right_logical(word, at) & ((1 << bits) - 1)

    def listing(b, n):
        words = [req_ref[b, s] for s in range(slots)]
        lengths = [jnp.where(w >= 0, length_ref[field(w, piece_bits, pass_bits)], 0) for w in words]
        for s, (word, length) in enumerate(zip(words, lengths)):
            cand_ref[pl.ds(b * slots + s, 1), :] = jnp.full((1, dim), req_ref[b, s + dim // 2], jnp.int32)
            for u in range(pieces):
                units_ref[n] = word + u
                n = n + jnp.where(length > u * UNIT, 1, 0)
        return n

    def place(t, part, swapped):
        peer = me ^ order[t] if order else t
        first = pl.multiple_of(peer * shard + core * half, 8)
        second = pl.multiple_of(peer * shard + half - core * half, 8)
        table_ref[pl.ds(first, half), :] = part[qrows : qrows + half, :].astype(jnp.float32)
        table_ref[pl.ds(second, half), :] = swapped[...].astype(jnp.float32)
        query_ref[pl.ds(pl.multiple_of(t * qrows, 16), qrows), :] = part[:qrows, :]

    def place_loop(t, carry):
        place(t, parts[0].at[t], other_ref.at[t])
        return carry

    if order:
        for t in range(peers):
            place(t, parts[t], other_ref.at[t])
    else:
        lax.fori_loop(0, peers, place_loop, 0)

    bring_req.wait()
    bring_length.wait()
    count = lax.fori_loop(0, peers, listing, 0)
    for u in range(GROUP):
        units_ref[count + u] = total << slot_at

    token = lax.broadcasted_iota(jnp.int32, (UNIT, qtok), 0)
    nt = (((1,), (1,)), ((), ()))

    pair = UNIT // 2

    def fetch(g, carry):
        for j in range(FETCH):
            unit = g * FETCH + j
            word = units_ref[unit]
            base = field(word, 0, piece_bits) * (pair * passages) + field(word, piece_bits, pass_bits)
            rows = rows_ref.at[pl.ds(pl.multiple_of(unit * UNIT, UNIT), UNIT)]
            for t in range(pair):
                codes = codes_ref[base + t * passages]
                rows[t : t + 1, :] = table_ref[pl.ds(codes & 0xFFFF, 1), :]
                rows[t + pair : t + pair + 1, :] = table_ref[pl.ds(lax.shift_right_logical(codes, 16), 1), :]
        return carry

    def compare(g, carry):
        found = []
        for j in range(GROUP):
            unit = g * GROUP + j
            word = units_ref[unit]
            piece = field(word, 0, piece_bits)
            p = field(word, piece_bits, pass_bits)
            row = piece * (total + 8) + field(word, slot_at, slot_bits)
            head = lax.shift_right_logical(word, head_at)
            resid = resid_ref[p, pl.ds(pl.multiple_of(piece * UNIT, UNIT), UNIT), :]
            query = query_ref[pl.ds(pl.multiple_of(head * qtok, qtok), qtok), :]
            left = length_ref[p] - piece * UNIT
            cent = rows_ref[pl.ds(pl.multiple_of(unit * UNIT, UNIT), UNIT), :]
            v = cent + resid.astype(jnp.float32)
            both = jnp.concatenate([normalize(v).astype(jnp.bfloat16), cent.astype(jnp.bfloat16)], axis=0)
            sims = lax.dot_general(both, query, nt, preferred_element_type=jnp.float32)
            tops = [
                jnp.max(jnp.where(token < left, sims[o : o + UNIT], -1000000000.0), axis=0, keepdims=True)
                for o in (0, UNIT)
            ]
            found.append((row, tops))
        for row, (exact, approx) in found:
            best_ref[pl.ds(row, 1), :] = exact
            near_ref[pl.ds(row, 1), :] = approx
        return carry

    bring_codes.wait()
    lax.fori_loop(0, (count + FETCH - 1) // FETCH, fetch, 0)
    bring_resid.wait()
    lax.fori_loop(0, (count + GROUP - 1) // GROUP, compare, 0)

    def score(ref):
        best = ref[:total, :]
        for u in range(1, pieces):
            best = jnp.maximum(best, ref[u * (total + 8) : u * (total + 8) + total, :])
        return jnp.sum(best, axis=1, keepdims=True)

    cand = cand_ref[...]
    lane = lax.broadcasted_iota(jnp.int32, (total, dim), 1)
    placed = jnp.where(lane == cand, score(best_ref), 0.0)
    placed += jnp.where(lane == cand + q_dev * per_query, score(near_ref), 0.0)
    placed = jnp.where(cand >= 0, placed, 0.0)
    placed = jnp.sum(placed.reshape(peers, slots, dim), axis=1)
    turned = [placed] + [pltpu.roll(placed, dim - r * per_query, 1) for r in range(1, 2 * q_dev)]
    for b in range(peers):
        to = me ^ order[b] if order else b
        for r in range(2 * q_dev):
            out_ref[to, r : r + 1, :] = turned[r][b : b + 1, :]


def body(queries, cand_owner, cand_local, centroids, passage_codes, residuals, passage_lengths):
    peers = lax.axis_size("index")
    cores = lax.axis_size("query")
    q_dev, per_query = cand_owner.shape
    count = q_dev * per_query
    slots = max(2, (2 * count + peers - 1) // peers)
    seq, dim = residuals.shape[1:]
    qtok = queries.shape[1]
    qrows = q_dev * qtok
    half = centroids.shape[0] // cores
    rows = qrows + half + PAD
    order = ORDER if peers == len(ORDER) else ()
    vmem = pl.BlockSpec(memory_space=pltpu.VMEM)
    smem = pl.BlockSpec(memory_space=pltpu.SMEM)
    hbm = pl.BlockSpec(memory_space=pltpu.HBM)
    copies = 1 if order else peers
    pack_mib = 2 * copies * rows * dim * 2 // MIB
    held = [passage_codes.T, passage_lengths]
    kept = [((seq // 2, residuals.shape[0]), jnp.int32), (passage_lengths.shape, jnp.int32)]
    inputs = [cand_owner, cand_local, queries, centroids] + held
    packed, *held = pl.pallas_call(
        pack_kernel,
        out_shape=[jax.ShapeDtypeStruct((copies, rows, dim), jnp.bfloat16)]
        + [jax.ShapeDtypeStruct(*x) for x in kept],
        in_specs=[hbm] * 6,
        out_specs=[vmem] * 3,
        scratch_shapes=[
            pltpu.VMEM(passage_codes.T.shape, jnp.int32),
            pltpu.SMEM((peers,), jnp.int32),
            pltpu.VMEM((peers + PAD, dim), jnp.float32),
            pltpu.SMEM(cand_owner.shape, jnp.int32),
            pltpu.SMEM(cand_local.shape, jnp.int32),
            pltpu.VMEM(queries.shape, queries.dtype),
            pltpu.VMEM((half, dim), centroids.dtype),
            pltpu.SemaphoreType.DMA((6,)),
        ],
        compiler_params=pltpu.CompilerParams(vmem_limit_bytes=(8 + pack_mib) * MIB),
    )(*(pltpu.with_memory_space_constraint(x, pltpu.HBM) for x in inputs))
    codes, lengths = held[0].reshape(-1), held[1]
    resid = pltpu.with_memory_space_constraint(residuals, pltpu.HBM)
    if order:
        swap = lambda x, t: lax.ppermute(x, "index", [(i, i ^ t) for i in range(peers)])
        known = {0: packed[0]}
        for t in order:
            if t not in known and t not in RELAYED:
                known[t] = swap(known[0], t)
        for t in RELAYED:
            known[t] = swap(known[t ^ 1], 1)
        parts = [known[t] for t in order]
        mine = jnp.stack([part[qrows : qrows + half] for part in parts])
        asked = jnp.stack([part[qrows + half :] for part in parts])
        asked = lax.dynamic_index_in_dim(asked, lax.axis_index("index"), 1, keepdims=False)
    else:
        parts = [lax.all_to_all(packed, "index", split_axis=0, concat_axis=0, tiled=True)]
        mine = parts[0][:, qrows : qrows + half]
        asked = parts[0][:, qrows + half]
    asked = asked.astype(jnp.int32)
    piece_bits, pass_bits, slot_bits = field_bits(peers, slots, residuals.shape[0], seq)
    place = jnp.arange(peers, dtype=jnp.int32)[:, None] * slots + jnp.arange(dim // 2, dtype=jnp.int32)[None]
    head = jnp.arange(peers, dtype=jnp.int32)[:, None] * q_dev + asked[:, dim // 2 :] // per_query
    word = ((((head << slot_bits) + place) << pass_bits) + asked[:, : dim // 2]) << piece_bits
    word = jnp.where(asked[:, : dim // 2] >= 0, word, -1)
    asked = jnp.concatenate([word, asked[:, dim // 2 :]], axis=1)
    other = lax.ppermute(mine, "query", [(0, 1), (1, 0)])
    table_mib = 2 * peers * half * dim * 2 // MIB
    bests = (seq // UNIT) * (peers * slots + 8)
    scores = pl.pallas_call(
        functools.partial(score_kernel, slots, q_dev, per_query, qtok, order),
        out_shape=jax.ShapeDtypeStruct((peers, 2 * q_dev, dim), jnp.float32),
        in_specs=[pl.BlockSpec(memory_space=pl.ANY)] * 3 + [vmem] * (len(parts) + 1) + [hbm],
        out_specs=vmem,
        scratch_shapes=[
            pltpu.VMEM((peers * qrows, dim), jnp.bfloat16),
            pltpu.VMEM((peers * cores * half, dim), jnp.float32),
            pltpu.VMEM((peers * slots * seq + GROUP * UNIT, dim), jnp.float32),
            pltpu.VMEM((bests, qtok), jnp.float32),
            pltpu.VMEM((bests, qtok), jnp.float32),
            pltpu.VMEM((peers * slots, dim), jnp.int32),
            pltpu.SMEM((peers * slots * (seq // UNIT) + GROUP,), jnp.int32),
            pltpu.SMEM(asked.shape, jnp.int32),
            pltpu.SMEM(lengths.shape, jnp.int32),
            pltpu.SMEM(codes.shape, jnp.int32),
            pltpu.VMEM(residuals.shape, residuals.dtype),
            pltpu.SemaphoreType.DMA((4,)),
        ],
        compiler_params=pltpu.CompilerParams(vmem_limit_bytes=(12 + 4 * table_mib + peers * slots * seq * dim * 4 // MIB) * MIB),
    )(asked, lengths, codes, *parts, other, resid)
    back = lax.all_to_all(scores, "index", split_axis=0, concat_axis=0, tiled=True)
    result = jnp.sum(back[:, :, :per_query], axis=0)
    return result[:q_dev], result[q_dev:]


def solution(mesh):
    in_specs = (
        P(("group", "index", "query"), None, None),
        P(("group", "index", "query"), None),
        P(("group", "index", "query"), None),
        P("index", None),
        P("index", None),
        P("index", None, None),
        P("index"),
    )
    out_specs = (P(("group", "index", "query"), None), P(("group", "index", "query"), None))
    return jax.shard_map(body, mesh=mesh, in_specs=in_specs, out_specs=out_specs, check_vma=False)
```

```python
import functools

import jax
import jax.numpy as jnp
from jax import lax
from jax.experimental import pallas as pl
from jax.experimental.pallas import tpu as pltpu
from jax.sharding import PartitionSpec as P

EPS = 1e-06
PAD = 16
UNIT = 32
GROUP = 48
ORDER = (4, 6, 1, 3, 2, 5, 7, 0)
RELAYED = (5, 7)
FETCH = 8
MIB = 1024 * 1024


def normalize(wide):
    return wide * lax.rsqrt(jnp.sum(wide * wide, axis=-1, keepdims=True) + EPS)


def pack_kernel(
    owner_hbm,
    local_hbm,
    queries_hbm,
    cent_hbm,
    codes_hbm,
    length_hbm,
    out_ref,
    codes_out,
    length_out,
    codes_ref,
    count_ref,
    req_ref,
    owner_ref,
    local_ref,
    queries_ref,
    cent_ref,
    sems,
):
    copies = out_ref.shape[0]
    peers = count_ref.shape[0]
    q_dev, per_query = owner_ref.shape
    qrows = queries_ref.shape[0] * queries_ref.shape[1]
    half, dim = cent_ref.shape
    core = lax.axis_index("query")
    cent_half = cent_hbm.at[pl.ds(pl.multiple_of(core * half, 16), half)]
    moves = [
        pltpu.make_async_copy(src, dst, sems.at[i])
        for i, (src, dst) in enumerate(
            (
                (owner_hbm, owner_ref),
                (local_hbm, local_ref),
                (queries_hbm, queries_ref),
                (cent_half, cent_ref),
                (codes_hbm, codes_ref),
                (length_hbm, length_out),
            )
        )
    ]
    for move in moves:
        move.start()

    def clear(i, carry):
        count_ref[i] = 0
        return carry

    lax.fori_loop(0, peers, clear, 0)
    for move in moves[:4]:
        move.wait()
    row = lax.broadcasted_iota(jnp.int32, req_ref.shape, 0)
    lane = lax.broadcasted_iota(jnp.int32, req_ref.shape, 1)
    req = jnp.full(req_ref.shape, -1, jnp.int32)
    for q in range(q_dev):
        for k in range(per_query):
            owner = owner_ref[q, k]
            slot = count_ref[owner]
            count_ref[owner] = slot + 1
            here = row == owner
            req = jnp.where(here & (lane == slot), local_ref[q, k], req)
            req = jnp.where(here & (lane == slot + dim // 2), q * per_query + k, req)
    req_ref[...] = req.astype(jnp.float32)
    qnorm = normalize(queries_ref[...].reshape(qrows, dim).astype(jnp.float32)).astype(jnp.bfloat16)

    def send(d, carry):
        out_ref[d, :qrows, :] = qnorm
        out_ref[d, qrows : qrows + half, :] = cent_ref[...]
        asked = req_ref[pl.ds(d, PAD), :]
        out_ref[d, qrows + half :, :] = asked.astype(jnp.bfloat16)
        return carry

    lax.fori_loop(0, copies, send, 0)
    for move in moves[4:]:
        move.wait()
    pair = UNIT // 2
    for u in range(codes_ref.shape[0] // UNIT):
        low = codes_ref[u * UNIT : u * UNIT + pair, :]
        high = codes_ref[u * UNIT + pair : (u + 1) * UNIT, :]
        codes_out[u * pair : (u + 1) * pair, :] = low | (high << 16)


def field_bits(peers, slots, passages, seq):
    return (seq // UNIT - 1).bit_length(), (passages - 1).bit_length(), (peers * slots).bit_length()


def score_kernel(slots, q_dev, per_query, qtok, order, req_any, length_any, codes_any, *refs):
    (*parts, other_ref, resid_hbm, out_ref) = refs[:-12]
    query_ref, table_ref, rows_ref, best_ref, near_ref, cand_ref, units_ref = refs[-12:-5]
    req_ref, length_ref, codes_ref, resid_ref, sems = refs[-5:]
    peers, half, dim = other_ref.shape
    qrows = q_dev * qtok
    passages, seq = resid_hbm.shape[:2]
    pieces = seq // UNIT
    shard = 2 * half
    total = peers * slots
    me = lax.axis_index("index")
    core = lax.axis_index("query")

    bring_req = pltpu.make_async_copy(req_any, req_ref, sems.at[0])
    bring_length = pltpu.make_async_copy(length_any, length_ref, sems.at[1])
    bring_codes = pltpu.make_async_copy(codes_any, codes_ref, sems.at[2])
    bring_resid = pltpu.make_async_copy(resid_hbm, resid_ref, sems.at[3])
    for bring in (bring_req, bring_length, bring_codes, bring_resid):
        bring.start()
    best_ref[...] = jnp.full(best_ref.shape, -1000000000.0, jnp.float32)
    near_ref[...] = jnp.full(near_ref.shape, -1000000000.0, jnp.float32)

    piece_bits, pass_bits, slot_bits = field_bits(peers, slots, passages, seq)
    cand_bits = (per_query - 1).bit_length()
    slot_at = piece_bits + pass_bits
    head_at = slot_at + slot_bits

    def field(word, at, bits):
        return lax.shift_right_logical(word, at) & ((1 << bits) - 1)

    def listing(b, n):
        words = [req_ref[b, s] for s in range(slots)]
        lengths = [jnp.where(w >= 0, length_ref[field(w, piece_bits, pass_bits)], 0) for w in words]
        for s, (word, length) in enumerate(zip(words, lengths)):
            cand_ref[pl.ds(b * slots + s, 1), :] = jnp.full((1, dim), req_ref[b, s + dim // 2], jnp.int32)
            for u in range(pieces):
                units_ref[n] = word + u
                n = n + jnp.where(length > u * UNIT, 1, 0)
        return n

    def place(t, part, swapped):
        peer = me ^ order[t] if order else t
        first = pl.multiple_of(peer * shard + core * half, 8)
        second = pl.multiple_of(peer * shard + half - core * half, 8)
        table_ref[pl.ds(first, half), :] = part[qrows : qrows + half, :].astype(jnp.float32)
        table_ref[pl.ds(second, half), :] = swapped[...].astype(jnp.float32)
        query_ref[pl.ds(pl.multiple_of(t * qrows, 16), qrows), :] = part[:qrows, :]

    def place_loop(t, carry):
        place(t, parts[0].at[t], other_ref.at[t])
        return carry

    if order:
        for t in range(peers):
            place(t, parts[t], other_ref.at[t])
    else:
        lax.fori_loop(0, peers, place_loop, 0)

    bring_req.wait()
    bring_length.wait()
    count = lax.fori_loop(0, peers, listing, 0)
    for u in range(GROUP):
        units_ref[count + u] = total << slot_at

    token = lax.broadcasted_iota(jnp.int32, (UNIT, qtok), 0)
    nt = (((1,), (1,)), ((), ()))

    pair = UNIT // 2

    def fetch(g, carry):
        for j in range(FETCH):
            unit = g * FETCH + j
            word = units_ref[unit]
            base = field(word, 0, piece_bits) * (pair * passages) + field(word, piece_bits, pass_bits)
            rows = rows_ref.at[pl.ds(pl.multiple_of(unit * UNIT, UNIT), UNIT)]
            for t in range(pair):
                codes = codes_ref[base + t * passages]
                rows[t : t + 1, :] = table_ref[pl.ds(codes & 0xFFFF, 1), :]
                rows[t + pair : t + pair + 1, :] = table_ref[pl.ds(lax.shift_right_logical(codes, 16), 1), :]
        return carry

    def compare(g, carry):
        found = []
        for j in range(GROUP):
            unit = g * GROUP + j
            word = units_ref[unit]
            piece = field(word, 0, piece_bits)
            p = field(word, piece_bits, pass_bits)
            row = piece * (total + 8) + field(word, slot_at, slot_bits)
            head = lax.shift_right_logical(word, head_at)
            resid = resid_ref[p, pl.ds(pl.multiple_of(piece * UNIT, UNIT), UNIT), :]
            query = query_ref[pl.ds(pl.multiple_of(head * qtok, qtok), qtok), :]
            left = length_ref[p] - piece * UNIT
            cent = rows_ref[pl.ds(pl.multiple_of(unit * UNIT, UNIT), UNIT), :]
            v = cent + resid.astype(jnp.float32)
            both = jnp.concatenate([normalize(v).astype(jnp.bfloat16), cent.astype(jnp.bfloat16)], axis=0)
            sims = lax.dot_general(both, query, nt, preferred_element_type=jnp.float32)
            tops = [
                jnp.max(jnp.where(token < left, sims[o : o + UNIT], -1000000000.0), axis=0, keepdims=True)
                for o in (0, UNIT)
            ]
            found.append((row, tops))
        for row, (exact, approx) in found:
            best_ref[pl.ds(row, 1), :] = exact
            near_ref[pl.ds(row, 1), :] = approx
        return carry

    bring_codes.wait()
    lax.fori_loop(0, (count + FETCH - 1) // FETCH, fetch, 0)
    bring_resid.wait()
    lax.fori_loop(0, (count + GROUP - 1) // GROUP, compare, 0)

    def score(ref):
        best = ref[:total, :]
        for u in range(1, pieces):
            best = jnp.maximum(best, ref[u * (total + 8) : u * (total + 8) + total, :])
        return jnp.sum(best, axis=1, keepdims=True)

    cand = cand_ref[...]
    lane = lax.broadcasted_iota(jnp.int32, (total, dim), 1)
    placed = jnp.where(lane == cand, score(best_ref), 0.0)
    placed += jnp.where(lane == cand + q_dev * per_query, score(near_ref), 0.0)
    placed = jnp.where(cand >= 0, placed, 0.0)
    placed = jnp.sum(placed.reshape(peers, slots, dim), axis=1)
    turned = [placed] + [pltpu.roll(placed, dim - r * per_query, 1) for r in range(1, 2 * q_dev)]
    for b in range(peers):
        to = me ^ order[b] if order else b
        for r in range(2 * q_dev):
            out_ref[to, r : r + 1, :] = turned[r][b : b + 1, :]


def body(queries, cand_owner, cand_local, centroids, passage_codes, residuals, passage_lengths):
    peers = lax.axis_size("index")
    cores = lax.axis_size("query")
    q_dev, per_query = cand_owner.shape
    count = q_dev * per_query
    slots = max(2, (2 * count + peers - 1) // peers)
    seq, dim = residuals.shape[1:]
    qtok = queries.shape[1]
    qrows = q_dev * qtok
    half = centroids.shape[0] // cores
    rows = qrows + half + PAD
    order = ORDER if peers == len(ORDER) else ()
    vmem = pl.BlockSpec(memory_space=pltpu.VMEM)
    smem = pl.BlockSpec(memory_space=pltpu.SMEM)
    hbm = pl.BlockSpec(memory_space=pltpu.HBM)
    copies = 1 if order else peers
    pack_mib = 2 * copies * rows * dim * 2 // MIB
    held = [passage_codes.T, passage_lengths]
    kept = [((seq // 2, residuals.shape[0]), jnp.int32), (passage_lengths.shape, jnp.int32)]
    inputs = [cand_owner, cand_local, queries, centroids] + held
    packed, *held = pl.pallas_call(
        pack_kernel,
        out_shape=[jax.ShapeDtypeStruct((copies, rows, dim), jnp.bfloat16)]
        + [jax.ShapeDtypeStruct(*x) for x in kept],
        in_specs=[hbm] * 6,
        out_specs=[vmem] * 3,
        scratch_shapes=[
            pltpu.VMEM(passage_codes.T.shape, jnp.int32),
            pltpu.SMEM((peers,), jnp.int32),
            pltpu.VMEM((peers + PAD, dim), jnp.float32),
            pltpu.SMEM(cand_owner.shape, jnp.int32),
            pltpu.SMEM(cand_local.shape, jnp.int32),
            pltpu.VMEM(queries.shape, queries.dtype),
            pltpu.VMEM((half, dim), centroids.dtype),
            pltpu.SemaphoreType.DMA((6,)),
        ],
        compiler_params=pltpu.CompilerParams(vmem_limit_bytes=(8 + pack_mib) * MIB),
    )(*(pltpu.with_memory_space_constraint(x, pltpu.HBM) for x in inputs))
    codes, lengths = held[0].reshape(-1), held[1]
    resid = pltpu.with_memory_space_constraint(residuals, pltpu.HBM)
    if order:
        swap = lambda x, t: lax.ppermute(x, "index", [(i, i ^ t) for i in range(peers)])
        known = {0: packed[0]}
        for t in order:
            if t not in known and t not in RELAYED:
                known[t] = swap(known[0], t)
        for t in RELAYED:
            known[t] = swap(known[t ^ 1], 1)
        parts = [known[t] for t in order]
        mine = jnp.stack([part[qrows : qrows + half] for part in parts])
        asked = jnp.stack([part[qrows + half :] for part in parts])
        asked = lax.dynamic_index_in_dim(asked, lax.axis_index("index"), 1, keepdims=False)
    else:
        parts = [lax.all_to_all(packed, "index", split_axis=0, concat_axis=0, tiled=True)]
        mine = parts[0][:, qrows : qrows + half]
        asked = parts[0][:, qrows + half]
    asked = asked.astype(jnp.int32)
    piece_bits, pass_bits, slot_bits = field_bits(peers, slots, residuals.shape[0], seq)
    place = jnp.arange(peers, dtype=jnp.int32)[:, None] * slots + jnp.arange(dim // 2, dtype=jnp.int32)[None]
    head = jnp.arange(peers, dtype=jnp.int32)[:, None] * q_dev + asked[:, dim // 2 :] // per_query
    word = ((((head << slot_bits) + place) << pass_bits) + asked[:, : dim // 2]) << piece_bits
    word = jnp.where(asked[:, : dim // 2] >= 0, word, -1)
    asked = jnp.concatenate([word, asked[:, dim // 2 :]], axis=1)
    other = lax.ppermute(mine, "query", [(0, 1), (1, 0)])
    table_mib = 2 * peers * half * dim * 2 // MIB
    bests = (seq // UNIT) * (peers * slots + 8)
    scores = pl.pallas_call(
        functools.partial(score_kernel, slots, q_dev, per_query, qtok, order),
        out_shape=jax.ShapeDtypeStruct((peers, 2 * q_dev, dim), jnp.float32),
        in_specs=[pl.BlockSpec(memory_space=pl.ANY)] * 3 + [vmem] * (len(parts) + 1) + [hbm],
        out_specs=vmem,
        scratch_shapes=[
            pltpu.VMEM((peers * qrows, dim), jnp.bfloat16),
            pltpu.VMEM((peers * cores * half, dim), jnp.float32),
            pltpu.VMEM((peers * slots * seq + GROUP * UNIT, dim), jnp.float32),
            pltpu.VMEM((bests, qtok), jnp.float32),
            pltpu.VMEM((bests, qtok), jnp.float32),
            pltpu.VMEM((peers * slots, dim), jnp.int32),
            pltpu.SMEM((peers * slots * (seq // UNIT) + GROUP,), jnp.int32),
            pltpu.SMEM(asked.shape, jnp.int32),
            pltpu.SMEM(lengths.shape, jnp.int32),
            pltpu.SMEM(codes.shape, jnp.int32),
            pltpu.VMEM(residuals.shape, residuals.dtype),
            pltpu.SemaphoreType.DMA((4,)),
        ],
        compiler_params=pltpu.CompilerParams(vmem_limit_bytes=(12 + 4 * table_mib + peers * slots * seq * dim * 4 // MIB) * MIB),
    )(asked, lengths, codes, *parts, other, resid)
    back = lax.all_to_all(scores, "index", split_axis=0, concat_axis=0, tiled=True)
    result = jnp.sum(back[:, :, :per_query], axis=0)
    return result[:q_dev], result[q_dev:]


def solution(mesh):
    in_specs = (
        P(("group", "index", "query"), None, None),
        P(("group", "index", "query"), None),
        P(("group", "index", "query"), None),
        P("index", None),
        P("index", None),
        P("index", None, None),
        P("index"),
    )
    out_specs = (P(("group", "index", "query"), None), P(("group", "index", "query"), None))
    return jax.shard_map(body, mesh=mesh, in_specs=in_specs, out_specs=out_specs, check_vma=False)
```
